512 devices in a mesh: band: 4 (over y), gx: 16 (over z), gy: 8 (over x, core).
Axes of the slice: x: 4, y: 4, z: 16, core: 2. Of those that a mesh axis runs over, the one named last changes fastest.
Arguments:
- psi_coeff: float32 [8, 256, 256, 256], P('band', 'gx', 'gy'), parts along dimension 0, may hold values from -6 to 6
- potential: float32 [256, 256, 256], P(('gx', 'gy')), may hold values from -15 to 15
- projectors: bfloat16 [2, 3, 256, 256, 256], P(None, None, 'gx', 'gy'), may hold values from -6 to 6
- coupling: float32 [2, 3, 3], replicated, may hold values from -6 to 6
- positions: float32 [3, 64], replicated, may hold values from 0 to 1
- species: int32 [64], replicated, may hold values from 0 to 1
Outputs:
- hpsi: float32 [8, 256, 256, 256], P('band', 'gx', 'gy'), parts along dimension 0
The draws below stay inside these ranges and needn't reach their ends.
There are 4 independent parts, one for each index of `band`. The reference program is written for one: setup_inputs(seed, part) draws one part's arguments, and reference() takes and returns one part's arrays. A program takes and returns all parts, laid end to end along the dimension named above; an argument that names none is the same for every part. Nothing has to cross between parts.
Inputs may be any that keep to these rules, and one draw needn't show every extreme that they name: species indices lie below 2.
All inputs are finite; a program needn't handle non-finite values.
Results may differ from the reference program's by a relative error of at most 0.00045.
Values sent between devices are 32-bit elements; how exact they have to be, the bound alone decides.
A program may use at most 64 MiB of HBM per device.

```python
import math
import jax
import jax.numpy as jnp
from jax import lax

NX = 256
NY = 256
NZ = 256
NSPEC = 2
LPROJ = 3
ATOMS = 64
N_GX = 16
N_GY = 8


def plant(values, rng, least, largest):
    longest = values.shape.index(max(values.shape))
    spots = []
    for shift in (0, 1):
        where = [jax.random.randint(jax.random.fold_in(rng, axis), (), 0, length) for axis, length in enumerate(values.shape)]
        where[longest] = (where[longest] + shift) % values.shape[longest]
        spots.append(tuple(where))
    return values.at[spots[0]].set(least).at[spots[1]].set(largest)


def steps_of(stream_key, shape, cuts, least, largest):
    def one(position, blocks):
        steps = jax.random.uniform(jax.random.fold_in(jax.random.fold_in(stream_key, 6), position), (blocks,), jnp.float32, least / len(cuts), largest / len(cuts))
        return jnp.repeat(jnp.exp(steps), shape[position] // blocks).reshape((-1,) + (1,) * (len(shape) - position - 1))

    level = one(*cuts[0])
    for cut in cuts[1:]:
        level = level * one(*cut)
    return level


def normal_values(own_key, extent, deviation, bound, pieces=(), kind=jnp.bfloat16):
    entries = deviation * jax.random.normal(own_key, extent, jnp.float32)
    if pieces:
        entries = entries * steps_of(own_key, extent, pieces, -0.22, 0.18)
    return jnp.clip(entries, -bound, bound).astype(kind)


def setup_inputs(seed: int = 0, part: int = 0) -> dict:
    splits = jax.random.split(jax.random.key(seed), 7)
    part_keys = jax.random.split(jax.random.fold_in(splits[6], part), 7)
    psi_coeff = normal_values(part_keys[0], (2, NX, NY, NZ), 1.0, 6.0, ((1, 16), (2, 8)), jnp.float32)
    potential = normal_values(splits[1], (NZ, NX, NY), 3.0, 15.0, ((0, 128),), jnp.float32)
    projectors = normal_values(splits[2], (NSPEC, LPROJ, NX, NY, NZ), 1.0, 6.0, ((2, 16), (3, 8)))
    coupling = normal_values(splits[3], (NSPEC, LPROJ, LPROJ), 1.0, 6.0, (), jnp.float32)
    positions = jnp.clip(jax.random.uniform(splits[4], (3, ATOMS), jnp.float32, 0.0, 1.0), 0.0, 1.0)
    species = plant(jax.random.randint(splits[5], (ATOMS,), 0, NSPEC), jax.random.fold_in(splits[5], 1), 0, NSPEC - 1).astype(jnp.int32)
    return {"psi_coeff": psi_coeff, "potential": potential, "projectors": projectors, "coupling": coupling, "positions": positions, "species": species}


TWO_PI = 2.0 * math.pi
HIGHEST = lax.Precision.HIGHEST

def signed_freq(count):
    index = jnp.arange(count, dtype=jnp.int32)
    return jnp.where(index < count // 2, index, index - count)

def axis_phase(freqs, coords):
    product = coords[:, None] * freqs[None, :].astype(coords.dtype)
    fraction = product - jnp.floor(product)
    angles = TWO_PI * fraction
    return (jnp.cos(angles), jnp.sin(angles))

def complex_einsum(einsum_form, left, right):
    left_re, left_im = left
    right_re, right_im = right

    def contract(first, second):
        return jnp.einsum(einsum_form, first, second, precision=HIGHEST)
    return (contract(left_re, right_re) - contract(left_im, right_im), contract(left_re, right_im) + contract(left_im, right_re))

def conjugate(pair):
    return (pair[0], -pair[1])

def row_of_freq(count, devices):
    freq = jnp.arange(count, dtype=jnp.int32)
    return freq % devices * (count // devices) + freq // devices

def freq_of_row(count, devices):
    row = jnp.arange(count, dtype=jnp.int32)
    block = count // devices
    return row // block + row % block * devices

def reference(psi_coeff, potential, projectors, coupling, positions, species):
    take_x = row_of_freq(NX, N_GX)
    take_y = row_of_freq(NY, N_GY)
    psi_coeff = jnp.take(jnp.take(psi_coeff, take_x, axis=1), take_y, axis=2)
    projectors = jnp.take(jnp.take(projectors, take_x, axis=2), take_y, axis=3)
    freq_x = signed_freq(NX)
    freq_y = signed_freq(NY)
    freq_z = signed_freq(NZ)
    squared = (freq_x * freq_x)[:, None, None] + (freq_y * freq_y)[None, :, None] + (freq_z * freq_z)[None, None, :]
    radius = min(NX, NY, NZ) // 4
    inside = squared <= radius * radius
    real_in = jnp.where(inside, psi_coeff[0], 0.0)
    imag_in = jnp.where(inside, psi_coeff[1], 0.0)
    cells = NX * NY * NZ
    root = math.sqrt(cells)
    wave = lax.complex(real_in, imag_in)
    space = jnp.fft.ifftn(wave) * root
    field = space * jnp.transpose(potential, (1, 2, 0))
    recip = jnp.fft.fftn(field) / root
    recip_re = jnp.real(recip).astype(jnp.float32)
    recip_im = jnp.imag(recip).astype(jnp.float32)
    species_table = (species[:, None] == jnp.arange(NSPEC, dtype=jnp.int32)[None, :]).astype(jnp.float32)
    phase_x = axis_phase(freq_x, positions[0])
    phase_y = axis_phase(freq_y, positions[1])
    phase_z = axis_phase(freq_z, positions[2])

    def plane_sum(index):
        plane = projectors[:, :, index].astype(jnp.float32)
        weighted = (plane * real_in[index], plane * imag_in[index])
        along_z = complex_einsum('sqyz,az->asqy', weighted, phase_z)
        return complex_einsum('asqy,ay->asq', along_z, phase_y)
    planes_re, planes_im = lax.map(plane_sum, jnp.arange(NX, dtype=jnp.int32))
    along_x = complex_einsum('xasq,ax->asq', (planes_re, planes_im), phase_x)
    proj_norm = 4.0 / root
    proj_re = jnp.einsum('as,asq->aq', species_table, along_x[0], precision=HIGHEST) * proj_norm
    proj_im = jnp.einsum('as,asq->aq', species_table, along_x[1], precision=HIGHEST) * proj_norm
    weight_re = jnp.einsum('as,sqm,am->aq', species_table, coupling, proj_re, precision=HIGHEST)
    weight_im = jnp.einsum('as,sqm,am->aq', species_table, coupling, proj_im, precision=HIGHEST)
    back_scale = 1.0 / math.sqrt(ATOMS * LPROJ)
    spread_re = species_table[:, :, None] * weight_re[:, None, :] * back_scale
    spread_im = species_table[:, :, None] * weight_im[:, None, :] * back_scale
    conj_y = conjugate(phase_y)
    conj_z = conjugate(phase_z)

    def plane_back(index):
        cos_x = phase_x[0][:, index]
        sin_x = -phase_x[1][:, index]
        start_re = spread_re * cos_x[:, None, None] - spread_im * sin_x[:, None, None]
        start_im = spread_re * sin_x[:, None, None] + spread_im * cos_x[:, None, None]
        back_y = complex_einsum('asq,ay->asqy', (start_re, start_im), conj_y)
        back_z = complex_einsum('asqy,az->sqyz', back_y, conj_z)
        plane = projectors[:, :, index].astype(jnp.float32)
        return (lax.optimization_barrier(jnp.sum(plane * back_z[0], axis=(0, 1))), lax.optimization_barrier(jnp.sum(plane * back_z[1], axis=(0, 1))))
    projector_re, projector_im = lax.map(plane_back, jnp.arange(NX, dtype=jnp.int32))
    kinetic = squared.astype(jnp.float32) / float(radius * radius)
    out_re = jnp.where(inside, kinetic * real_in + recip_re + projector_re, 0.0)
    out_im = jnp.where(inside, kinetic * imag_in + recip_im + projector_im, 0.0)
    result = jnp.stack((out_re, out_im))
    result = jnp.take(result, freq_of_row(NX, N_GX), axis=1)
    return jnp.take(result, freq_of_row(NY, N_GY), axis=2)
```

```python
import functools
import math

import jax
import jax.numpy as jnp
import ml_dtypes
import numpy as np
from jax import lax
from jax.experimental import pallas as pl
from jax.experimental.pallas import tpu as pltpu
from jax.sharding import PartitionSpec as P

MESH = pl.DeviceIdType.MESH
N = 256
GX = 16
GY = 8
COLS = 128
RADIUS = 64
ATOMS = 64
NSPEC = 2
LPROJ = 3
TWO_PI = 2.0 * math.pi
ROWS_X = (0, 1, 2, 3, 12, 13, 14, 15)
HELD_X = (0, 1, 2, 3, 5, 6, 7, 8)
COL_Y = 71
COL_X = 72


def column_offsets(col):
    a = col // 16
    b = col % 16
    a = a - 8 * (a >= 4)
    b = b - 16 * (b >= 8)
    a = np.where(col == COL_Y, 0, np.where(col == COL_X, 4, a))
    b = np.where(col == COL_Y, 8, np.where(col == COL_X, 0, b))
    return a, b


def two_parts(table):
    table = table.astype(np.float32)
    high = table.astype(ml_dtypes.bfloat16)
    low = (table - high.astype(np.float32)).astype(ml_dtypes.bfloat16)
    return np.stack([high, low])


@functools.lru_cache(maxsize=None)
def tables():
    t, g, c, y = np.meshgrid(
        np.arange(2), np.arange(GX), np.arange(2), np.arange(GY), indexing="ij"
    )
    z = (16 * g + 2 * y + t).reshape(-1, 1)
    c = c.reshape(-1, 1)
    angle = TWO_PI / N * (z * np.arange(N)[None, :] % N)
    cos, sin = np.cos(angle) / 16, np.sin(angle) / 16
    tz = np.concatenate(
        [np.where(c == 0, cos, sin), np.where(c == 0, -sin, cos)], axis=1
    )
    a, b = column_offsets(np.arange(COLS))
    x0 = np.repeat(np.arange(16), 32)[None, :]
    y0 = np.tile(np.arange(32), 16)[None, :]
    angle = TWO_PI * ((2 * a[:, None] * x0 + b[:, None] * y0) % 32) / 32
    cos, sin = np.cos(angle) / 16, np.sin(angle) / 16
    t1 = np.block([[cos, sin], [-sin, cos]])
    gy = np.repeat(np.arange(GY), GX)[:, None]
    gx = np.tile(np.arange(GX), GY)[:, None]
    angle = TWO_PI * ((gx * x0 + gy * y0) % N) / N
    t2 = np.stack([np.cos(angle), np.sin(angle)]).astype(np.float32)
    y1, x1 = gy, gx
    angle = TWO_PI * ((gx.T * x1 + 2 * gy.T * y1) % 16) / 16
    cos, sin = np.cos(angle) / 16, np.sin(angle) / 16
    e = np.block([[cos, -sin], [sin, cos]])
    return (
        two_parts(tz),
        two_parts(t1),
        two_parts(t1.T),
        np.concatenate([two_parts(e), two_parts(e.T)]),
        t2,
    )


def split(value):
    high = value.astype(jnp.bfloat16)
    return high, (value - high.astype(jnp.float32)).astype(jnp.bfloat16)


def product(left, right, dims=((1,), (0,))):
    def one(first, second):
        return lax.dot_general(
            first, second, (dims, ((), ())), preferred_element_type=jnp.float32
        )

    return one(left[0], right[0]) + (one(left[0], right[1]) + one(left[1], right[0]))


def cos_turns(turns):
    r = (turns - jnp.floor(turns + 0.5)) * math.pi
    r2 = r * r
    s = -1.0 / 39916800.0
    for denom in (362880.0, -5040.0, 120.0, -6.0, 1.0):
        s = s * r2 + 1.0 / denom
    s = s * r
    return 1.0 - 2.0 * s * s


def iota(shape, axis):
    return lax.broadcasted_iota(jnp.int32, shape, axis)


def column_freqs(gx, gy, shape):
    col = iota(shape, 0)
    a = lax.shift_right_logical(col, 4)
    b = col & 15
    a = jnp.where(a >= 4, a - 8, a)
    b = jnp.where(b >= 8, b - 16, b)
    a = jnp.where(col == COL_Y, 0, jnp.where(col == COL_X, 4, a))
    b = jnp.where(col == COL_Y, 8, jnp.where(col == COL_X, 0, b))
    return gx + GX * a, gy + GY * b


def fractional(product_):
    return product_ - jnp.floor(product_)


def pick_columns(held):
    tiles = []
    for place, i in enumerate(HELD_X):
        row = held(i)
        first, second = row[0:8], row[24:32]
        if place == 4:
            sub = iota((8, N), 0)
            other = jnp.broadcast_to(held(0)[8:9], (8, N))
            first = jnp.where(sub == 7, other, first)
            other = jnp.broadcast_to(held(4)[0:1], (8, N))
            second = jnp.where(sub == 0, other, second)
        tiles += [first, second]
    return jnp.concatenate(tiles, axis=0)


def kernel(
    psi_h, pot_h, proj_h, coup, pos, spec, tz_h, t1_h, t1t_h, e_h, t2_h,
    out,
    psi, pot, proj, tz, t1, t1t, e, t2,
    xs, pf, pz, pxy, vt, nl,
    zs, r1, s2, r2, s3, r3, s4, r4, ar0, ar1, ar2,
    load_sem, sx, rx, sy, ry,
):
    gx = lax.axis_index("gx")
    gy = lax.axis_index("gy")
    loads = []
    pairs = [
        (psi_h.at[:, 0:5], psi.at[:, 0:5]),
        (psi_h.at[:, 12:16], psi.at[:, 5:9]),
        (tz_h, tz),
        (proj_h.at[:, :, 0:5], proj.at[:, :, 0:5]),
        (proj_h.at[:, :, 12:16], proj.at[:, :, 5:9]),
        (pot_h.at[:, :, 0:128], pot.at[0]),
        (pot_h.at[:, :, 128:256], pot.at[1]),
        (t1_h, t1),
        (t2_h, t2),
        (e_h, e),
        (t1t_h, t1t),
    ]
    for i, (src, dst) in enumerate(pairs):
        loads.append(pltpu.make_async_copy(src, dst, load_sem.at[i]))
        loads[-1].start()

    barrier = pltpu.get_barrier_semaphore()

    @pl.loop(1, GX)
    def _(d):
        pl.semaphore_signal(
            barrier, inc=1, device_id={"gx": lax.rem(gx + d, GX)}, device_id_type=MESH
        )

    @pl.loop(1, GY)
    def _(d):
        pl.semaphore_signal(
            barrier, inc=1, device_id={"gy": lax.rem(gy + d, GY)}, device_id_type=MESH
        )

    def over_x(slot, d, source, target):
        peer = lax.rem(gx + d, GX)
        return pltpu.make_async_remote_copy(
            src_ref=source(peer),
            dst_ref=target(gx),
            send_sem=sx.at[slot, d],
            recv_sem=rx.at[slot, d],
            device_id={"gx": peer},
            device_id_type=MESH,
        )

    def over_y(slot, d, source, target):
        peer = lax.rem(gy + d, GY)
        return pltpu.make_async_remote_copy(
            src_ref=source(peer),
            dst_ref=target(gy),
            send_sem=sy.at[slot, d],
            recv_sem=ry.at[slot, d],
            device_id={"gy": peer},
            device_id_type=MESH,
        )

    def send(over, count, slot, source, target):
        @pl.loop(1, count)
        def _(d):
            over(slot, d, source, target).start()

    def receive(over, count, slot, source, target):
        @pl.loop(1, count)
        def _(d):
            over(slot, d, source, target).wait()

    def rows16(i):
        return pl.ds(pl.multiple_of(i * 16, 16), 16)

    def rows32(i):
        return pl.ds(pl.multiple_of(i * 32, 32), 32)

    kx, ky = column_freqs(gx, gy, (COLS, N))
    lane = iota((COLS, N), 1)
    kz = jnp.where(lane < N // 2, lane, lane - N)
    squared = kx * kx + ky * ky + kz * kz
    inside = squared <= RADIUS * RADIUS
    kinetic = squared.astype(jnp.float32) * (1.0 / (RADIUS * RADIUS))
    loads[0].wait()
    loads[1].wait()
    for c in range(2):
        xs[c] = jnp.where(inside, pick_columns(lambda i: psi[c, i]), 0.0)
    x_parts = split(jnp.concatenate([xs[0], xs[1]], axis=1))
    loads[2].wait()

    def tz_parts(t):
        rows = pl.ds(256 * t, 256)
        return tz[0, rows, :], tz[1, rows, :]

    p1 = [(lambda p, t=t: zs.at[t, p], lambda m, t=t: r1.at[t, rows16(m)]) for t in range(2)]
    p2 = [(lambda p, t=t: s2.at[t, p], lambda m, t=t: r2.at[t, m]) for t in range(2)]
    p3 = [(lambda p, t=t: s3.at[t, p], lambda m, t=t: r3.at[t, rows32(m)]) for t in range(2)]
    p4 = [(lambda p, t=t: s4.at[t, p], lambda m, t=t: r4.at[t, m]) for t in range(2)]

    for t in range(2):
        lines = product(tz_parts(t), x_parts, ((1,), (1,)))
        zs[t] = lines.reshape(GX, 16, COLS)
        if t == 0:
            pl.semaphore_wait(barrier, GX + GY - 2)
        send(over_x, GX, t, *p1[t])
        r1[t, rows16(gx), :] = zs[t, gx]

    atoms2 = jnp.concatenate([pos[...], pos[...]], axis=1)
    half = iota((1, 2 * ATOMS), 1) >= ATOMS
    quarter = jnp.where(half, 0.25, 0.0)
    row = iota((N, 2 * ATOMS), 0)
    kz_rows = jnp.where(row < N // 2, row, row - N).astype(jnp.float32)
    turns_z = fractional(kz_rows * atoms2[2:3])
    pz_f32 = jnp.concatenate(
        [cos_turns(turns_z - quarter), cos_turns(turns_z + (0.25 - quarter))], axis=0
    )
    pz[0], pz[1] = split(pz_f32)
    kx_col, ky_col = column_freqs(gx, gy, (COLS, 2 * ATOMS))
    turns_xy = fractional(kx_col.astype(jnp.float32) * atoms2[0:1]) + fractional(
        ky_col.astype(jnp.float32) * atoms2[1:2]
    )
    pxy[0] = cos_turns(turns_xy)
    pxy[1] = cos_turns(turns_xy + jnp.where(half, -0.25, 0.25))

    loads[3].wait()
    loads[4].wait()
    pz_parts = (pz[0], pz[1])
    sums = []
    for s in range(NSPEC):
        for q in range(LPROJ):
            factor = pick_columns(lambda i: proj[s, q, i].astype(jnp.float32))
            pf[s * LPROJ + q] = factor
            weighted = jnp.concatenate([factor * xs[0], factor * xs[1]], axis=1)
            along_z = product(split(weighted), pz_parts)
            along = along_z * pxy[0] + pltpu.roll(along_z, ATOMS, 1) * pxy[1]
            sums.append(jnp.sum(along, axis=0, keepdims=True))
    species = jnp.concatenate([spec[...], spec[...]], axis=1)
    norm = 4.0 / math.sqrt(N * N * N)
    sub = iota((8, 2 * ATOMS), 0)
    part = jnp.zeros((8, 2 * ATOMS), jnp.float32)
    for q in range(LPROJ):
        chosen = jnp.where(species == 0, sums[q], sums[LPROJ + q]) * norm
        part = jnp.where(sub == q, chosen, part)
    ar0[0] = part
    ar1[gx] = part
    a1 = (lambda p: ar0.at[0], lambda m: ar1.at[m])
    a2 = (lambda p: ar0.at[1], lambda m: ar2.at[m])
    send(over_x, GX, 4, *a1)

    loads[5].wait()
    loads[6].wait()
    lane16 = iota((16, 128), 1)
    for t in range(2):
        for block in range(4):
            for hy in range(2):
                strips = [
                    pot[hy, t, pl.ds(4 * block + j, 16, stride=16), :] for j in range(4)
                ]
                for r in range(4):
                    tile = None
                    for j in range(4):
                        shift = (32 * (j - r)) % 128
                        moved = strips[j] if shift == 0 else pltpu.roll(strips[j], shift, 1)
                        tile = moved if tile is None else jnp.where(lane16 >= 32 * j, moved, tile)
                    y1 = 4 * hy + r
                    vt[t, pl.ds(16 * y1, 16), pl.ds(128 * block, 128)] = tile

    def pass_on(t):
        receive(over_x, GX, t, *p1[t])
        for g in range(GY):
            for c in range(2):
                s2[t, g, pl.ds(16 * c, 16), :] = r1[t, pl.ds(8 * c + g, 16, stride=16), :]
        send(over_y, GY, t, *p2[t])
        r2[t, gy] = s2[t, gy]

    def plane(t):
        receive(over_y, GY, t, *p2[t])
        values = jnp.concatenate(
            [r2[t, :, 0:16, :].reshape(COLS, COLS), r2[t, :, 16:32, :].reshape(COLS, COLS)],
            axis=1,
        )
        lanes = product(split(values), (t1[0], t1[1]))
        lanes_re, lanes_im = lanes[:, :512], lanes[:, 512:]
        cos, sin = t2[0], t2[1]
        turned = jnp.concatenate(
            [lanes_re * cos - lanes_im * sin, lanes_re * sin + lanes_im * cos], axis=0
        )
        space = product((e[0], e[1]), split(turned))
        field = jnp.concatenate([space[:128] * vt[t], space[128:] * vt[t]], axis=0)
        rows = product((e[2], e[3]), split(field))
        rows_re, rows_im = rows[:128], rows[128:]
        turned = jnp.concatenate(
            [rows_re * cos + rows_im * sin, rows_im * cos - rows_re * sin], axis=1
        )
        back = product(split(turned), (t1t[0], t1t[1]))
        s3[t, :, 0:16, :] = back[:, :128].reshape(GY, 16, COLS)
        s3[t, :, 16:32, :] = back[:, 128:].reshape(GY, 16, COLS)
        send(over_y, GY, 2 + t, *p3[t])
        r3[t, rows32(gy), :] = s3[t, gy]

    def return_on(t):
        receive(over_y, GY, 2 + t, *p3[t])
        for g in range(GX):
            for c in range(2):
                s4[t, g, pl.ds(8 * c, 8), :] = r3[t, pl.ds(16 * c + g, 8, stride=32), :]
        send(over_x, GX, 2 + t, *p4[t])
        r4[t, gx] = s4[t, gx]

    pass_on(0)
    receive(over_x, GX, 4, *a1)
    total = ar1[0]
    for g in range(1, GX):
        total += ar1[g]
    ar0[1] = total
    ar2[gy] = total
    send(over_y, GY, 4, *a2)
    for i in range(7, 11):
        loads[i].wait()
    plane(0)
    pass_on(1)
    return_on(0)
    plane(1)
    return_on(1)

    receive(over_y, GY, 4, *a2)
    total = ar2[0]
    for g in range(1, GY):
        total += ar2[g]
    spread = []
    for s in range(NSPEC):
        for q in range(LPROJ):
            weight = coup[s, q, 0] * total[0:1]
            for m in range(1, LPROJ):
                weight += coup[s, q, m] * total[m : m + 1]
            weight = weight * (1.0 / math.sqrt(ATOMS * LPROJ))
            spread.append(jnp.where(species == s, weight, 0.0))
    nonloc = None
    for i, weight in enumerate(spread):
        around = pltpu.roll(jnp.broadcast_to(weight, (8, 2 * ATOMS)), ATOMS, 1)[0:1]
        at_columns = pxy[0] * weight - pxy[1] * around
        spread_z = product(split(at_columns), pz_parts, ((1,), (1,)))
        term = jnp.concatenate([pf[i] * spread_z[:, :N], pf[i] * spread_z[:, N:]], axis=1)
        nonloc = term if nonloc is None else nonloc + term
    for c in range(2):
        nl[c] = nonloc[:, c * N : (c + 1) * N] + kinetic * xs[c]

    recip = None
    for t in range(2):
        receive(over_x, GX, 2 + t, *p4[t])
        lines = r4[t].reshape(256, COLS)
        term = product(split(jnp.transpose(lines)), tz_parts(t))
        recip = term if recip is None else recip + term
    for c in range(2):
        out[c] = jnp.where(inside, nl[c] + recip[:, c * N : (c + 1) * N], 0.0)


def place(columns, out):
    sub = iota((8, N), 0)
    for c in range(2):
        for row in range(16):
            if row in ROWS_X:
                base = 16 * ROWS_X.index(row)
                out[c, row, 0:8, :] = columns[c, base : base + 8, :]
                out[c, row, 8:24, :] = jnp.zeros((16, N), jnp.float32)
                out[c, row, 24:32, :] = columns[c, base + 8 : base + 16, :]
            else:
                out[c, row] = jnp.zeros((32, N), jnp.float32)
        along_y = jnp.broadcast_to(columns[c, COL_Y : COL_Y + 1, :], (8, N))
        out[c, 0, 8:16, :] = jnp.where(sub == 0, along_y, 0.0)
        along_x = jnp.broadcast_to(columns[c, COL_X : COL_X + 1, :], (8, N))
        out[c, 4, 0:8, :] = jnp.where(sub == 0, along_x, 0.0)
        corner = columns[c, 64:72, :]
        out[c, 12, 0:8, :] = jnp.where(sub == 7, 0.0, corner)
        corner = columns[c, 72:80, :]
        out[c, 12, 24:32, :] = jnp.where(sub == 0, 0.0, corner)


def per_device(psi_coeff, potential, projectors, coupling, positions, species):
    f32, bf16 = jnp.float32, jnp.bfloat16
    consts = [jnp.asarray(table) for table in tables()]
    hbm = pl.BlockSpec(memory_space=pl.ANY)
    vmem = pl.BlockSpec(memory_space=pltpu.VMEM)
    smem = pl.BlockSpec(memory_space=pltpu.SMEM)
    columns = pl.pallas_call(
        kernel,
        out_shape=jax.ShapeDtypeStruct((2, COLS, N), f32),
        in_specs=[hbm, hbm, hbm, smem, vmem, vmem] + [hbm] * 5,
        out_specs=vmem,
        scratch_shapes=[
            pltpu.VMEM((2, 9, 32, N), f32),
            pltpu.VMEM((2, 2, N, 128), f32),
            pltpu.VMEM((NSPEC, LPROJ, 9, 32, N), bf16),
            pltpu.VMEM((2, 512, 512), bf16),
            pltpu.VMEM((2, 256, 1024), bf16),
            pltpu.VMEM((2, 1024, 256), bf16),
            pltpu.VMEM((4, 256, 256), bf16),
            pltpu.VMEM((2, 128, 512), f32),
            pltpu.VMEM((2, COLS, N), f32),
            pltpu.VMEM((NSPEC * LPROJ, COLS, N), f32),
            pltpu.VMEM((2, 2 * N, 2 * ATOMS), bf16),
            pltpu.VMEM((2, COLS, 2 * ATOMS), f32),
            pltpu.VMEM((2, 128, 512), f32),
            pltpu.VMEM((2, COLS, N), f32),
            pltpu.VMEM((2, GX, 16, COLS), f32),
            pltpu.VMEM((2, GX * 16, COLS), f32),
            pltpu.VMEM((2, GY, 32, COLS), f32),
            pltpu.VMEM((2, GY, 32, COLS), f32),
            pltpu.VMEM((2, GY, 32, COLS), f32),
            pltpu.VMEM((2, GY * 32, COLS), f32),
            pltpu.VMEM((2, GX, 16, COLS), f32),
            pltpu.VMEM((2, GX, 16, COLS), f32),
            pltpu.VMEM((2, 8, 128), f32),
            pltpu.VMEM((GX, 8, 128), f32),
            pltpu.VMEM((GY, 8, 128), f32),
            pltpu.SemaphoreType.DMA((11,)),
            pltpu.SemaphoreType.DMA((5, GX)),
            pltpu.SemaphoreType.DMA((5, GX)),
            pltpu.SemaphoreType.DMA((5, GY)),
            pltpu.SemaphoreType.DMA((5, GY)),
        ],
        compiler_params=pltpu.CompilerParams(
            collective_id=0, has_side_effects=True, vmem_limit_bytes=48 * 1024 * 1024
        ),
    )(psi_coeff, potential, projectors, coupling, positions, species.reshape(1, ATOMS), *consts)
    return pl.pallas_call(
        place,
        out_shape=jax.ShapeDtypeStruct((2, 16, 32, N), f32),
        in_specs=[vmem],
        out_specs=vmem,
    )(columns)


def solution(mesh):
    in_specs = (
        P("band", "gx", "gy", None),
        P(("gx", "gy"), None, None),
        P(None, None, "gx", "gy", None),
        P(),
        P(),
        P(),
    )
    out_specs = P("band", "gx", "gy", None)
    return jax.shard_map(
        per_device, mesh=mesh, in_specs=in_specs, out_specs=out_specs, check_vma=False
    )
```

```python
import functools
import math

import jax
import jax.numpy as jnp
import ml_dtypes
import numpy as np
from jax import lax
from jax.experimental import pallas as pl
from jax.experimental.pallas import tpu as pltpu
from jax.sharding import PartitionSpec as P

MESH = pl.DeviceIdType.MESH
N = 256
GX = 16
GY = 8
COLS = 128
RADIUS = 64
ATOMS = 64
NSPEC = 2
LPROJ = 3
TWO_PI = 2.0 * math.pi
ROWS_X = (0, 1, 2, 3, 12, 13, 14, 15)
HELD_X = (0, 1, 2, 3, 5, 6, 7, 8)
COL_Y = 71
COL_X = 72


def column_offsets(col):
    a = col // 16
    b = col % 16
    a = a - 8 * (a >= 4)
    b = b - 16 * (b >= 8)
    a = np.where(col == COL_Y, 0, np.where(col == COL_X, 4, a))
    b = np.where(col == COL_Y, 8, np.where(col == COL_X, 0, b))
    return a, b


def two_parts(table):
    table = table.astype(np.float32)
    high = table.astype(ml_dtypes.bfloat16)
    low = (table - high.astype(np.float32)).astype(ml_dtypes.bfloat16)
    return np.stack([high, low])


@functools.lru_cache(maxsize=None)
def tables():
    t, g, c, y = np.meshgrid(
        np.arange(2), np.arange(GX), np.arange(2), np.arange(GY), indexing="ij"
    )
    z = (16 * g + 2 * y + t).reshape(-1, 1)
    c = c.reshape(-1, 1)
    angle = TWO_PI / N * (z * np.arange(N)[None, :] % N)
    cos, sin = np.cos(angle) / 16, np.sin(angle) / 16
    tz = np.concatenate(
        [np.where(c == 0, cos, sin), np.where(c == 0, -sin, cos)], axis=1
    )
    a, b = column_offsets(np.arange(COLS))
    x0 = np.repeat(np.arange(16), 32)[None, :]
    y0 = np.tile(np.arange(32), 16)[None, :]
    angle = TWO_PI * ((2 * a[:, None] * x0 + b[:, None] * y0) % 32) / 32
    cos, sin = np.cos(angle) / 16, np.sin(angle) / 16
    t1 = np.block([[cos, sin], [-sin, cos]])
    gy = np.repeat(np.arange(GY), GX)[:, None]
    gx = np.tile(np.arange(GX), GY)[:, None]
    angle = TWO_PI * ((gx * x0 + gy * y0) % N) / N
    t2 = np.stack([np.cos(angle), np.sin(angle)]).astype(np.float32)
    y1, x1 = gy, gx
    angle = TWO_PI * ((gx.T * x1 + 2 * gy.T * y1) % 16) / 16
    cos, sin = np.cos(angle) / 16, np.sin(angle) / 16
    e = np.block([[cos, -sin], [sin, cos]])
    return (
        two_parts(tz),
        two_parts(t1),
        two_parts(t1.T),
        np.concatenate([two_parts(e), two_parts(e.T)]),
        t2,
    )


def split(value):
    high = value.astype(jnp.bfloat16)
    return high, (value - high.astype(jnp.float32)).astype(jnp.bfloat16)


def product(left, right, dims=((1,), (0,))):
    def one(first, second):
        return lax.dot_general(
            first, second, (dims, ((), ())), preferred_element_type=jnp.float32
        )

    return one(left[0], right[0]) + (one(left[0], right[1]) + one(left[1], right[0]))


def cos_turns(turns):
    r = (turns - jnp.floor(turns + 0.5)) * math.pi
    r2 = r * r
    s = -1.0 / 39916800.0
    for denom in (362880.0, -5040.0, 120.0, -6.0, 1.0):
        s = s * r2 + 1.0 / denom
    s = s * r
    return 1.0 - 2.0 * s * s


def iota(shape, axis):
    return lax.broadcasted_iota(jnp.int32, shape, axis)


def column_freqs(gx, gy, shape):
    col = iota(shape, 0)
    a = lax.shift_right_logical(col, 4)
    b = col & 15
    a = jnp.where(a >= 4, a - 8, a)
    b = jnp.where(b >= 8, b - 16, b)
    a = jnp.where(col == COL_Y, 0, jnp.where(col == COL_X, 4, a))
    b = jnp.where(col == COL_Y, 8, jnp.where(col == COL_X, 0, b))
    return gx + GX * a, gy + GY * b


def fractional(product_):
    return product_ - jnp.floor(product_)


def pick_columns(held):
    tiles = []
    for place, i in enumerate(HELD_X):
        row = held(i)
        first, second = row[0:8], row[24:32]
        if place == 4:
            sub = iota((8, N), 0)
            other = jnp.broadcast_to(held(0)[8:9], (8, N))
            first = jnp.where(sub == 7, other, first)
            other = jnp.broadcast_to(held(4)[0:1], (8, N))
            second = jnp.where(sub == 0, other, second)
        tiles += [first, second]
    return jnp.concatenate(tiles, axis=0)


def kernel(
    psi_h, pot_h, proj_h, coup_h, pos_h, spec_h, tz_h, t1_h, t1t_h, e_h, t2_h,
    out,
    psi, pot, proj, coup, pos, spec, tz, t1, t1t, e, t2,
    xs, pf, pz, pxy, vt, nl,
    zs, r1, s2, r2, s3, r3, s4, r4, ar0, ar1, ar2,
    load_sem, sems,
):
    gx = lax.axis_index("gx")
    gy = lax.axis_index("gy")
    loads = []
    pairs = [
        (psi_h.at[:, 0:5], psi.at[:, 0:5]),
        (psi_h.at[:, 12:16], psi.at[:, 5:9]),
        (tz_h, tz),
        (proj_h.at[:, :, 0:5], proj.at[:, :, 0:5]),
        (proj_h.at[:, :, 12:16], proj.at[:, :, 5:9]),
        (pot_h.at[:, :, 0:128], pot.at[0]),
        (pot_h.at[:, :, 128:256], pot.at[1]),
        (t1_h, t1),
        (t2_h, t2),
        (e_h, e),
        (t1t_h, t1t),
        (pos_h, pos),
        (spec_h, spec),
        (coup_h, coup),
    ]
    for i, (src, dst) in enumerate(pairs):
        loads.append(pltpu.make_async_copy(src, dst, load_sem.at[i]))
        loads[-1].start()

    barrier = pltpu.get_barrier_semaphore()

    @pl.loop(1, GX)
    def _(d):
        pl.semaphore_signal(
            barrier, inc=1, device_id={"gx": lax.rem(gx + d, GX)}, device_id_type=MESH
        )

    @pl.loop(1, GY)
    def _(d):
        pl.semaphore_signal(
            barrier, inc=1, device_id={"gy": lax.rem(gy + d, GY)}, device_id_type=MESH
        )

    def exchange(axis, me, count, slot, source, target, block, landing):
        send_sem, recv_sem = sems.at[2 * slot], sems.at[2 * slot + 1]

        def post(d):
            peer = lax.rem(me + d, count)
            pltpu.make_async_remote_copy(
                src_ref=source(peer),
                dst_ref=target(me),
                send_sem=send_sem,
                recv_sem=recv_sem,
                device_id={axis: peer},
                device_id_type=MESH,
            ).start()

        for k in range(1, count):
            d = count // 2 - k // 2 if k % 2 == 1 else count // 2 + k // 2
            post(d)
        pltpu.make_async_copy(source(me), target(me), recv_sem).start()

        def sent():
            pltpu.make_async_copy(block, block, send_sem).wait()

        def landed():
            pltpu.make_async_copy(landing, landing, recv_sem).wait()

        return sent, landed

    def over_x(*args):
        return exchange("gx", gx, GX, *args)

    def over_y(*args):
        return exchange("gy", gy, GY, *args)

    def rows16(i):
        return pl.ds(pl.multiple_of(i * 16, 16), 16)

    def rows32(i):
        return pl.ds(pl.multiple_of(i * 32, 32), 32)

    kx, ky = column_freqs(gx, gy, (COLS, N))
    lane = iota((COLS, N), 1)
    kz = jnp.where(lane < N // 2, lane, lane - N)
    squared = kx * kx + ky * ky + kz * kz
    inside = squared <= RADIUS * RADIUS
    kinetic = squared.astype(jnp.float32) * (1.0 / (RADIUS * RADIUS))
    loads[0].wait()
    loads[1].wait()
    for c in range(2):
        xs[c] = jnp.where(inside, pick_columns(lambda i: psi[c, i]), 0.0)
    x_parts = split(jnp.concatenate([xs[0], xs[1]], axis=1))
    loads[2].wait()

    def tz_parts(t):
        rows = pl.ds(256 * t, 256)
        return tz[0, rows, :], tz[1, rows, :]

    few_x, few_y = pl.ds(0, GX - 1), pl.ds(0, GY - 1)

    def post1(t):
        return over_x(
            t, lambda p: zs.at[t, p], lambda m: r1.at[t, rows16(m)],
            zs.at[t, few_x], r1.at[t],
        )

    def lines(t):
        zs[t] = product(tz_parts(t), x_parts, ((1,), (1,))).reshape(GX, 16, COLS)

    lines(0)
    pl.semaphore_wait(barrier, GX + GY - 2)
    sent1, landed1 = [None, None], [None, None]
    sent1[0], landed1[0] = post1(0)
    lines(1)
    loads[11].wait()
    loads[12].wait()
    loads[13].wait()
    atoms2 = jnp.concatenate([pos[...], pos[...]], axis=1)
    half = iota((1, 2 * ATOMS), 1) >= ATOMS
    quarter = jnp.where(half, 0.25, 0.0)
    row = iota((N, 2 * ATOMS), 0)
    kz_rows = jnp.where(row < N // 2, row, row - N).astype(jnp.float32)
    turns_z = fractional(kz_rows * atoms2[2:3])
    pz_f32 = jnp.concatenate(
        [cos_turns(turns_z - quarter), cos_turns(turns_z + (0.25 - quarter))], axis=0
    )
    pz[0], pz[1] = split(pz_f32)
    kx_col, ky_col = column_freqs(gx, gy, (COLS, 2 * ATOMS))
    turns_xy = fractional(kx_col.astype(jnp.float32) * atoms2[0:1]) + fractional(
        ky_col.astype(jnp.float32) * atoms2[1:2]
    )
    pxy[0] = cos_turns(turns_xy)
    pxy[1] = cos_turns(turns_xy + jnp.where(half, -0.25, 0.25))

    loads[3].wait()
    loads[4].wait()
    pz_parts = (pz[0], pz[1])
    sums = []
    for s in range(NSPEC):
        for q in range(LPROJ):
            factor = pick_columns(lambda i: proj[s, q, i].astype(jnp.float32))
            pf[s * LPROJ + q] = factor
            weighted = jnp.concatenate([factor * xs[0], factor * xs[1]], axis=1)
            along_z = product(split(weighted), pz_parts)
            along = along_z * pxy[0] + pltpu.roll(along_z, ATOMS, 1) * pxy[1]
            sums.append(jnp.sum(along, axis=0, keepdims=True))
    species = jnp.concatenate([spec[...], spec[...]], axis=1)
    norm = 4.0 / math.sqrt(N * N * N)
    sub = iota((8, 2 * ATOMS), 0)
    part = jnp.zeros((8, 2 * ATOMS), jnp.float32)
    for q in range(LPROJ):
        chosen = jnp.where(species == 0, sums[q], sums[LPROJ + q]) * norm
        part = jnp.where(sub == q, chosen, part)
    ar0[0] = part
    sent_a1, landed_a1 = over_x(
        8, lambda p: ar0.at[0], lambda m: ar1.at[m], ar1.at[few_x], ar1
    )

    loads[5].wait()
    loads[6].wait()
    lane16 = iota((16, 128), 1)
    for t in range(2):
        for block in range(4):
            for hy in range(2):
                strips = [
                    pot[hy, t, pl.ds(4 * block + j, 16, stride=16), :] for j in range(4)
                ]
                for r in range(4):
                    tile = None
                    for j in range(4):
                        shift = (32 * (j - r)) % 128
                        moved = strips[j] if shift == 0 else pltpu.roll(strips[j], shift, 1)
                        tile = moved if tile is None else jnp.where(lane16 >= 32 * j, moved, tile)
                    y1 = 4 * hy + r
                    vt[t, pl.ds(16 * y1, 16), pl.ds(128 * block, 128)] = tile

    sent1[0]()
    sent1[0] = lambda: None
    sent1[1], landed1[1] = post1(1)

    def pass_on(t):
        landed1[t]()
        for g in range(GY):
            for c in range(2):
                s2[t, g, pl.ds(16 * c, 16), :] = r1[t, pl.ds(8 * c + g, 16, stride=16), :]
        return over_y(
            2 + t, lambda p: s2.at[t, p], lambda m: r2.at[t, m], s2.at[t, few_y], r2.at[t]
        )

    def plane(t):
        landed2[t]()
        values = jnp.concatenate(
            [r2[t, :, 0:16, :].reshape(COLS, COLS), r2[t, :, 16:32, :].reshape(COLS, COLS)],
            axis=1,
        )
        lanes = product(split(values), (t1[0], t1[1]))
        lanes_re, lanes_im = lanes[:, :512], lanes[:, 512:]
        cos, sin = t2[0], t2[1]
        turned = jnp.concatenate(
            [lanes_re * cos - lanes_im * sin, lanes_re * sin + lanes_im * cos], axis=0
        )
        space = product((e[0], e[1]), split(turned))
        field = jnp.concatenate([space[:128] * vt[t], space[128:] * vt[t]], axis=0)
        rows = product((e[2], e[3]), split(field))
        rows_re, rows_im = rows[:128], rows[128:]
        turned = jnp.concatenate(
            [rows_re * cos + rows_im * sin, rows_im * cos - rows_re * sin], axis=1
        )
        back = product(split(turned), (t1t[0], t1t[1]))
        s3[t, :, 0:16, :] = back[:, :128].reshape(GY, 16, COLS)
        s3[t, :, 16:32, :] = back[:, 128:].reshape(GY, 16, COLS)
        return over_y(
            4 + t, lambda p: s3.at[t, p], lambda m: r3.at[t, rows32(m)],
            s3.at[t, few_y], r3.at[t],
        )

    def return_on(t):
        landed3[t]()
        for g in range(GX):
            for c in range(2):
                s4[t, g, pl.ds(8 * c, 8), :] = r3[t, pl.ds(16 * c + g, 8, stride=32), :]
        return over_x(
            6 + t, lambda p: s4.at[t, p], lambda m: r4.at[t, m], s4.at[t, few_x], r4.at[t]
        )

    sent2, landed2 = [None, None], [None, None]
    sent3, landed3 = [None, None], [None, None]
    sent4, landed4 = [None, None], [None, None]
    sent2[0], landed2[0] = pass_on(0)
    landed_a1()
    total = ar1[0]
    for g in range(1, GX):
        total += ar1[g]
    ar0[1] = total
    sent_a2, landed_a2 = over_y(
        9, lambda p: ar0.at[1], lambda m: ar2.at[m], ar2.at[few_y], ar2
    )
    for i in range(7, 11):
        loads[i].wait()
    sent3[0], landed3[0] = plane(0)
    sent2[1], landed2[1] = pass_on(1)
    sent4[0], landed4[0] = return_on(0)
    sent3[1], landed3[1] = plane(1)
    sent4[1], landed4[1] = return_on(1)

    landed_a2()
    total = ar2[0]
    for g in range(1, GY):
        total += ar2[g]
    spread = []
    for s in range(NSPEC):
        for q in range(LPROJ):
            weight = coup[q, s : s + 1, 0:1] * total[0:1]
            for m in range(1, LPROJ):
                weight += coup[q, s : s + 1, m : m + 1] * total[m : m + 1]
            weight = weight * (1.0 / math.sqrt(ATOMS * LPROJ))
            spread.append(jnp.where(species == s, weight, 0.0))
    nonloc = None
    for i, weight in enumerate(spread):
        around = pltpu.roll(jnp.broadcast_to(weight, (8, 2 * ATOMS)), ATOMS, 1)[0:1]
        at_columns = pxy[0] * weight - pxy[1] * around
        spread_z = product(split(at_columns), pz_parts, ((1,), (1,)))
        term = jnp.concatenate([pf[i] * spread_z[:, :N], pf[i] * spread_z[:, N:]], axis=1)
        nonloc = term if nonloc is None else nonloc + term
    for c in range(2):
        nl[c] = nonloc[:, c * N : (c + 1) * N] + kinetic * xs[c]

    recip = None
    for t in range(2):
        landed4[t]()
        lines = r4[t].reshape(256, COLS)
        term = product(split(jnp.transpose(lines)), tz_parts(t))
        recip = term if recip is None else recip + term
    for c in range(2):
        out[c] = jnp.where(inside, nl[c] + recip[:, c * N : (c + 1) * N], 0.0)
    for sent in (*sent1, *sent2, *sent3, *sent4, sent_a1, sent_a2):
        sent()


def place(columns, out):
    sub = iota((8, N), 0)
    for c in range(2):
        for row in range(16):
            if row in ROWS_X:
                base = 16 * ROWS_X.index(row)
                out[c, row, 0:8, :] = columns[c, base : base + 8, :]
                out[c, row, 8:24, :] = jnp.zeros((16, N), jnp.float32)
                out[c, row, 24:32, :] = columns[c, base + 8 : base + 16, :]
            else:
                out[c, row] = jnp.zeros((32, N), jnp.float32)
        along_y = jnp.broadcast_to(columns[c, COL_Y : COL_Y + 1, :], (8, N))
        out[c, 0, 8:16, :] = jnp.where(sub == 0, along_y, 0.0)
        along_x = jnp.broadcast_to(columns[c, COL_X : COL_X + 1, :], (8, N))
        out[c, 4, 0:8, :] = jnp.where(sub == 0, along_x, 0.0)
        corner = columns[c, 64:72, :]
        out[c, 12, 0:8, :] = jnp.where(sub == 7, 0.0, corner)
        corner = columns[c, 72:80, :]
        out[c, 12, 24:32, :] = jnp.where(sub == 0, 0.0, corner)


def per_device(psi_coeff, potential, projectors, coupling, positions, species):
    f32, bf16 = jnp.float32, jnp.bfloat16
    consts = [jnp.asarray(table) for table in tables()]
    hbm = pl.BlockSpec(memory_space=pltpu.HBM)
    vmem = pl.BlockSpec(memory_space=pltpu.VMEM)
    columns = pl.pallas_call(
        kernel,
        out_shape=jax.ShapeDtypeStruct((2, COLS, N), f32),
        in_specs=[hbm] * 11,
        out_specs=vmem,
        scratch_shapes=[
            pltpu.VMEM((2, 9, 32, N), f32),
            pltpu.VMEM((2, 2, N, 128), f32),
            pltpu.VMEM((NSPEC, LPROJ, 9, 32, N), bf16),
            pltpu.VMEM((LPROJ, NSPEC, LPROJ), f32),
            pltpu.VMEM((3, ATOMS), f32),
            pltpu.VMEM((1, ATOMS), jnp.int32),
            pltpu.VMEM((2, 512, 512), bf16),
            pltpu.VMEM((2, 256, 1024), bf16),
            pltpu.VMEM((2, 1024, 256), bf16),
            pltpu.VMEM((4, 256, 256), bf16),
            pltpu.VMEM((2, 128, 512), f32),
            pltpu.VMEM((2, COLS, N), f32),
            pltpu.VMEM((NSPEC * LPROJ, COLS, N), f32),
            pltpu.VMEM((2, 2 * N, 2 * ATOMS), bf16),
            pltpu.VMEM((2, COLS, 2 * ATOMS), f32),
            pltpu.VMEM((2, 128, 512), f32),
            pltpu.VMEM((2, COLS, N), f32),
            pltpu.VMEM((2, GX, 16, COLS), f32),
            pltpu.VMEM((2, GX * 16, COLS), f32),
            pltpu.VMEM((2, GY, 32, COLS), f32),
            pltpu.VMEM((2, GY, 32, COLS), f32),
            pltpu.VMEM((2, GY, 32, COLS), f32),
            pltpu.VMEM((2, GY * 32, COLS), f32),
            pltpu.VMEM((2, GX, 16, COLS), f32),
            pltpu.VMEM((2, GX, 16, COLS), f32),
            pltpu.VMEM((2, 8, 128), f32),
            pltpu.VMEM((GX, 8, 128), f32),
            pltpu.VMEM((GY, 8, 128), f32),
            pltpu.SemaphoreType.DMA((14,)),
            pltpu.SemaphoreType.DMA((20,)),
        ],
        compiler_params=pltpu.CompilerParams(
            collective_id=0, has_side_effects=True, vmem_limit_bytes=60 * 1024 * 1024
        ),
    )(
        psi_coeff,
        potential,
        projectors,
        jnp.transpose(coupling, (1, 0, 2)),
        positions,
        species.reshape(1, ATOMS),
        *consts,
    )
    return pl.pallas_call(
        place,
        out_shape=jax.ShapeDtypeStruct((2, 16, 32, N), f32),
        in_specs=[vmem],
        out_specs=vmem,
    )(columns)


def solution(mesh):
    in_specs = (
        P("band", "gx", "gy", None),
        P(("gx", "gy"), None, None),
        P(None, None, "gx", "gy", None),
        P(),
        P(),
        P(),
    )
    out_specs = P("band", "gx", "gy", None)
    return jax.shard_map(
        per_device, mesh=mesh, in_specs=in_specs, out_specs=out_specs, check_vma=False
    )
```

```python
import functools
import math

import jax
import jax.numpy as jnp
import ml_dtypes
import numpy as np
from jax import lax
from jax.experimental import pallas as pl
from jax.experimental.pallas import tpu as pltpu
from jax.sharding import PartitionSpec as P

MESH = pl.DeviceIdType.MESH
N = 256
GX = 16
GY = 8
COLS = 128
RADIUS = 64
ATOMS = 64
NSPEC = 2
LPROJ = 3
TWO_PI = 2.0 * math.pi
ROWS_X = (0, 1, 2, 3, 12, 13, 14, 15)
HELD_X = (0, 1, 2, 3, 5, 6, 7, 8)
COL_Y = 71
COL_X = 72


def column_offsets(col):
    a = col // 16
    b = col % 16
    a = a - 8 * (a >= 4)
    b = b - 16 * (b >= 8)
    a = np.where(col == COL_Y, 0, np.where(col == COL_X, 4, a))
    b = np.where(col == COL_Y, 8, np.where(col == COL_X, 0, b))
    return a, b


def two_parts(table):
    table = table.astype(np.float32)
    high = table.astype(ml_dtypes.bfloat16)
    low = (table - high.astype(np.float32)).astype(ml_dtypes.bfloat16)
    return np.stack([high, low])


@functools.lru_cache(maxsize=None)
def tables():
    t, g, y, c = np.meshgrid(
        np.arange(2), np.arange(GX), np.arange(GY), np.arange(2), indexing="ij"
    )
    z = (16 * g + 2 * y + t).reshape(-1, 1)
    c = c.reshape(-1, 1)
    angle = TWO_PI / N * (z * np.arange(N)[None, :] % N)
    cos, sin = np.cos(angle) / 16, np.sin(angle) / 16
    tz = np.concatenate(
        [np.where(c == 0, cos, sin), np.where(c == 0, -sin, cos)], axis=1
    )
    a, b = column_offsets(np.arange(COLS))
    x0 = np.repeat(np.arange(16), 32)[None, :]
    y0 = np.tile(np.arange(32), 16)[None, :]
    angle = TWO_PI * ((2 * a[:, None] * x0 + b[:, None] * y0) % 32) / 32
    cos, sin = np.cos(angle) / 16, np.sin(angle) / 16
    t1 = np.block([[cos, sin], [-sin, cos]])
    gy = np.repeat(np.arange(GY), GX)[:, None]
    gx = np.tile(np.arange(GX), GY)[:, None]
    angle = TWO_PI * ((gx * x0 + gy * y0) % N) / N
    t2 = np.stack([np.cos(angle), np.sin(angle)]).astype(np.float32)
    y1, x1 = gy, gx
    angle = TWO_PI * ((gx.T * x1 + 2 * gy.T * y1) % 16) / 16
    cos, sin = np.cos(angle) / 16, np.sin(angle) / 16
    e = np.block([[cos, -sin], [sin, cos]])
    return (
        two_parts(tz),
        two_parts(t1),
        two_parts(t1.T),
        np.concatenate([two_parts(e), two_parts(e.T)]),
        t2,
    )


def split(value):
    high = value.astype(jnp.bfloat16)
    return high, (value - high.astype(jnp.float32)).astype(jnp.bfloat16)


def product(left, right, dims=((1,), (0,))):
    def one(first, second):
        return lax.dot_general(
            first, second, (dims, ((), ())), preferred_element_type=jnp.float32
        )

    return one(left[0], right[0]) + (one(left[0], right[1]) + one(left[1], right[0]))


def cos_turns(turns):
    r = (turns - jnp.floor(turns + 0.5)) * math.pi
    r2 = r * r
    s = -1.0 / 39916800.0
    for denom in (362880.0, -5040.0, 120.0, -6.0, 1.0):
        s = s * r2 + 1.0 / denom
    s = s * r
    return 1.0 - 2.0 * s * s


def iota(shape, axis):
    return lax.broadcasted_iota(jnp.int32, shape, axis)


def column_freqs(gx, gy, shape):
    col = iota(shape, 0)
    a = lax.shift_right_logical(col, 4)
    b = col & 15
    a = jnp.where(a >= 4, a - 8, a)
    b = jnp.where(b >= 8, b - 16, b)
    a = jnp.where(col == COL_Y, 0, jnp.where(col == COL_X, 4, a))
    b = jnp.where(col == COL_Y, 8, jnp.where(col == COL_X, 0, b))
    return gx + GX * a, gy + GY * b


def fractional(product_):
    return product_ - jnp.floor(product_)


def pick_columns(held):
    tiles = []
    for place, i in enumerate(HELD_X):
        row = held(i)
        first, second = row[0:8], row[24:32]
        if place == 4:
            sub = iota((8, N), 0)
            other = jnp.broadcast_to(held(0)[8:9], (8, N))
            first = jnp.where(sub == 7, other, first)
            other = jnp.broadcast_to(held(4)[0:1], (8, N))
            second = jnp.where(sub == 0, other, second)
        tiles += [first, second]
    return jnp.concatenate(tiles, axis=0)


def kernel(
    psi_h, pot_h, proj_h, coup_h, pos_h, spec_h, tz_h, t1_h, t1t_h, e_h, t2_h,
    out,
    psi, pot, proj, coup, pos, spec, tz, t1, t1t, e, t2,
    xs, pf, pz, pxy, vt, nl,
    zs, r2, s3, r4, ar0, ar1, ar2,
    load_sem, sems, ready,
):
    gx = lax.axis_index("gx")
    gy = lax.axis_index("gy")
    loads = []
    pairs = [
        (psi_h.at[:, 0:5], psi.at[:, 0:5]),
        (psi_h.at[:, 12:16], psi.at[:, 5:9]),
        (tz_h, tz),
        (proj_h.at[:, :, 0:5], proj.at[:, :, 0:5]),
        (proj_h.at[:, :, 12:16], proj.at[:, :, 5:9]),
        (pot_h.at[:, :, 0:128], pot.at[0]),
        (pot_h.at[:, :, 128:256], pot.at[1]),
        (t1_h, t1),
        (t2_h, t2),
        (e_h, e),
        (t1t_h, t1t),
        (pos_h, pos),
        (spec_h, spec),
        (coup_h, coup),
    ]
    for i, (src, dst) in enumerate(pairs):
        loads.append(pltpu.make_async_copy(src, dst, load_sem.at[i]))
    for load in loads[:3]:
        load.start()
    barrier = pltpu.get_barrier_semaphore()
    for d in range(1, GX):
        pl.semaphore_signal(
            barrier, inc=1, device_id={"gx": lax.rem(gx + d, GX)}, device_id_type=MESH
        )
    for d in range(1, GY):
        pl.semaphore_signal(
            barrier, inc=1, device_id={"gy": lax.rem(gy + d, GY)}, device_id_type=MESH
        )
    for load in loads[3:]:
        load.start()

    def exchange(axis, me, count, slot, source, target, block, landing):
        send_sem, recv_sem = sems.at[2 * slot], sems.at[2 * slot + 1]

        def post(d):
            peer = lax.rem(me + d, count)
            pltpu.make_async_remote_copy(
                src_ref=source(peer),
                dst_ref=target(me),
                send_sem=send_sem,
                recv_sem=recv_sem,
                device_id={axis: peer},
                device_id_type=MESH,
            ).start()

        for k in range(1, count):
            d = count // 2 - k // 2 if k % 2 == 1 else count // 2 + k // 2
            post(d)
        pltpu.make_async_copy(source(me), target(me), recv_sem).start()

        def sent():
            pltpu.make_async_copy(block, block, send_sem).wait()

        def landed():
            pltpu.make_async_copy(landing, landing, recv_sem).wait()

        return sent, landed

    def over_x(*args):
        return exchange("gx", gx, GX, *args)

    def over_y(*args):
        return exchange("gy", gy, GY, *args)

    by_x = [lax.rem(gx + d, GX) for d in range(GX)]
    by_y = [lax.rem(gy + d, GY) for d in range(GY)]

    def exchange_all(slot, source, target, source_at, target_at):
        send_sem, recv_sem = sems.at[2 * slot], sems.at[2 * slot + 1]
        mine = target.at[pl.ds(target_at(gx, gy), 2), :]

        def post(px, py):
            pltpu.make_async_remote_copy(
                src_ref=source.at[pl.ds(source_at(px, py), 2), :],
                dst_ref=mine,
                send_sem=send_sem,
                recv_sem=recv_sem,
                device_id={"gx": px, "gy": py},
                device_id_type=MESH,
            ).start()

        for py in by_y:
            post(by_x[8], py)

        @pl.loop(1, 8)
        def _(j):
            one, other = lax.rem(gx + (8 - j), GX), lax.rem(gx + (8 + j), GX)
            for py in by_y:
                post(one, py)
                post(other, py)

        for py in by_y[1:]:
            post(gx, py)
        pltpu.make_async_copy(
            source.at[pl.ds(source_at(gx, gy), 2), :], mine, recv_sem
        ).start()

        def sent():
            block = source.at[pl.ds(0, 254), :]
            pltpu.make_async_copy(block, block, send_sem).wait()

        def landed():
            pltpu.make_async_copy(target, target, recv_sem).wait()

        return sent, landed

    def by_gx(px, py):
        return (px * GY + py) * 2

    def by_gy(px, py):
        return (py * GX + px) * 2

    kx, ky = column_freqs(gx, gy, (COLS, N))
    lane = iota((COLS, N), 1)
    kz = jnp.where(lane < N // 2, lane, lane - N)
    squared = kx * kx + ky * ky + kz * kz
    inside = squared <= RADIUS * RADIUS
    kinetic = squared.astype(jnp.float32) * (1.0 / (RADIUS * RADIUS))
    loads[0].wait()
    loads[1].wait()
    for c in range(2):
        xs[c] = jnp.where(inside, pick_columns(lambda i: psi[c, i]), 0.0)
    x_parts = split(jnp.concatenate([xs[0], xs[1]], axis=1))
    loads[2].wait()

    def tz_parts(t):
        rows = pl.ds(256 * t, 256)
        return tz[0, rows, :], tz[1, rows, :]

    few_x, few_y = pl.ds(0, GX - 1), pl.ds(0, GY - 1)

    def lines(t):
        zs[t] = product(tz_parts(t), x_parts, ((1,), (1,)))

    def scatter(t):
        return exchange_all(t, zs.at[t], r2.at[t], by_gx, by_gy)

    lines(0)
    pl.semaphore_wait(barrier, GX + GY - 2)
    for py in by_y[1:]:
        pl.semaphore_signal(ready, inc=1, device_id={"gy": py}, device_id_type=MESH)
    lines(1)
    pl.semaphore_wait(ready, GY - 1)
    sent1, landed1 = [None, None], [None, None]
    sent1[0], landed1[0] = scatter(0)

    loads[11].wait()
    loads[12].wait()
    loads[13].wait()
    atoms2 = jnp.concatenate([pos[...], pos[...]], axis=1)
    half = iota((1, 2 * ATOMS), 1) >= ATOMS
    quarter = jnp.where(half, 0.25, 0.0)
    row = iota((N, 2 * ATOMS), 0)
    kz_rows = jnp.where(row < N // 2, row, row - N).astype(jnp.float32)
    turns_z = fractional(kz_rows * atoms2[2:3])
    pz_f32 = jnp.concatenate(
        [cos_turns(turns_z - quarter), cos_turns(turns_z + (0.25 - quarter))], axis=0
    )
    pz[0], pz[1] = split(pz_f32)
    kx_col, ky_col = column_freqs(gx, gy, (COLS, 2 * ATOMS))
    turns_xy = fractional(kx_col.astype(jnp.float32) * atoms2[0:1]) + fractional(
        ky_col.astype(jnp.float32) * atoms2[1:2]
    )
    pxy[0] = cos_turns(turns_xy)
    pxy[1] = cos_turns(turns_xy + jnp.where(half, -0.25, 0.25))

    loads[3].wait()
    loads[4].wait()
    pz_parts = (pz[0], pz[1])
    sums = []
    for s in range(NSPEC):
        for q in range(LPROJ):
            factor = pick_columns(lambda i: proj[s, q, i].astype(jnp.float32))
            pf[s * LPROJ + q] = factor
            weighted = jnp.concatenate([factor * xs[0], factor * xs[1]], axis=1)
            along_z = product(split(weighted), pz_parts)
            along = along_z * pxy[0] + pltpu.roll(along_z, ATOMS, 1) * pxy[1]
            sums.append(jnp.sum(along, axis=0, keepdims=True))
    species = jnp.concatenate([spec[...], spec[...]], axis=1)
    norm = 4.0 / math.sqrt(N * N * N)
    sub = iota((8, 2 * ATOMS), 0)
    part = jnp.zeros((8, 2 * ATOMS), jnp.float32)
    for q in range(LPROJ):
        chosen = jnp.where(species == 0, sums[q], sums[LPROJ + q]) * norm
        part = jnp.where(sub == q, chosen, part)
    ar0[0] = part
    sent_a1, landed_a1 = over_x(
        4, lambda p: ar0.at[0], lambda m: ar1.at[m], ar1.at[few_x], ar1
    )

    loads[5].wait()
    loads[6].wait()
    lane16 = iota((16, 128), 1)
    for t in range(2):
        for block in range(4):
            for hy in range(2):
                strips = [
                    pot[hy, t, pl.ds(4 * block + j, 16, stride=16), :] for j in range(4)
                ]
                for r in range(4):
                    tile = None
                    for j in range(4):
                        shift = (32 * (j - r)) % 128
                        moved = strips[j] if shift == 0 else pltpu.roll(strips[j], shift, 1)
                        tile = moved if tile is None else jnp.where(lane16 >= 32 * j, moved, tile)
                    y1 = 4 * hy + r
                    vt[t, pl.ds(16 * y1, 16), pl.ds(128 * block, 128)] = tile

    sent1[0]()
    sent1[1], landed1[1] = scatter(1)

    def plane(t):
        landed1[t]()
        values = jnp.concatenate(
            [r2[t, pl.ds(0, COLS, stride=2), :], r2[t, pl.ds(1, COLS, stride=2), :]], axis=1
        )
        lanes = product(split(values), (t1[0], t1[1]))
        lanes_re, lanes_im = lanes[:, :512], lanes[:, 512:]
        cos, sin = t2[0], t2[1]
        turned = jnp.concatenate(
            [lanes_re * cos - lanes_im * sin, lanes_re * sin + lanes_im * cos], axis=0
        )
        space = product((e[0], e[1]), split(turned))
        field = jnp.concatenate([space[:128] * vt[t], space[128:] * vt[t]], axis=0)
        rows = product((e[2], e[3]), split(field))
        rows_re, rows_im = rows[:128], rows[128:]
        turned = jnp.concatenate(
            [rows_re * cos + rows_im * sin, rows_im * cos - rows_re * sin], axis=1
        )
        back = product(split(turned), (t1t[0], t1t[1]))
        s3[t, pl.ds(0, COLS, stride=2), :] = back[:, :128]
        s3[t, pl.ds(1, COLS, stride=2), :] = back[:, 128:]

    def gather(t):
        return exchange_all(2 + t, s3.at[t], r4.at[t], by_gy, by_gx)

    sent4, landed4 = [None, None], [None, None]
    landed_a1()
    total = ar1[0]
    for g in range(1, GX):
        total += ar1[g]
    ar0[1] = total
    sent_a2, landed_a2 = over_y(
        5, lambda p: ar0.at[1], lambda m: ar2.at[m], ar2.at[few_y], ar2
    )
    for i in range(7, 11):
        loads[i].wait()
    plane(0)
    sent4[0], landed4[0] = gather(0)
    plane(1)
    sent4[1], landed4[1] = gather(1)

    landed_a2()
    total = ar2[0]
    for g in range(1, GY):
        total += ar2[g]
    spread = []
    for s in range(NSPEC):
        for q in range(LPROJ):
            weight = coup[q, s : s + 1, 0:1] * total[0:1]
            for m in range(1, LPROJ):
                weight += coup[q, s : s + 1, m : m + 1] * total[m : m + 1]
            weight = weight * (1.0 / math.sqrt(ATOMS * LPROJ))
            spread.append(jnp.where(species == s, weight, 0.0))
    nonloc = None
    for i, weight in enumerate(spread):
        around = pltpu.roll(jnp.broadcast_to(weight, (8, 2 * ATOMS)), ATOMS, 1)[0:1]
        at_columns = pxy[0] * weight - pxy[1] * around
        spread_z = product(split(at_columns), pz_parts, ((1,), (1,)))
        term = jnp.concatenate([pf[i] * spread_z[:, :N], pf[i] * spread_z[:, N:]], axis=1)
        nonloc = term if nonloc is None else nonloc + term
    for c in range(2):
        nl[c] = nonloc[:, c * N : (c + 1) * N] + kinetic * xs[c]

    recip = None
    for t in range(2):
        landed4[t]()
        term = product(split(jnp.transpose(r4[t])), tz_parts(t))
        recip = term if recip is None else recip + term
    for c in range(2):
        value = jnp.where(inside, nl[c] + recip[:, c * N : (c + 1) * N], 0.0)
        col = iota((COLS, N), 0)
        corner = (col == COL_X) | (col == COL_Y)
        regular = jnp.where(corner, 0.0, value).reshape(8, 2, 8, N)
        sub = iota((8, N), 0)
        for half in range(2):
            out[c, pl.ds(8 * half, 8)] = regular[:, half]
        for place, special in ((16, COL_X), (17, COL_Y)):
            row = jnp.broadcast_to(value[special : special + 1], (8, N))
            out[c, place] = jnp.where(sub == 0, row, 0.0)
    for sent in (sent1[1], *sent4, sent_a1, sent_a2):
        sent()


def place(tiles, out, held, zeros, load_sem, sem):
    load = pltpu.make_async_copy(tiles, held, load_sem)
    load.start()
    copies = []

    def put(src, dst):
        copies.append(pltpu.make_async_copy(src, dst, sem.at[len(copies)]))
        copies[-1].start()

    zeros[...] = jnp.zeros_like(zeros)
    for c in range(2):
        put(zeros, out.at[c, 5:12])
        put(zeros.at[0, 8:32], out.at[c, 4, 8:32])
        put(zeros.at[0:3, 8:24], out.at[c, 1:4, 8:24])
        put(zeros.at[0:4, 8:24], out.at[c, 12:16, 8:24])
        put(zeros.at[0, 16:24], out.at[c, 0, 16:24])
    load.wait()
    for half, rows in enumerate((pl.ds(0, 8), pl.ds(24, 8))):
        put(held.at[:, pl.ds(8 * half, 4)], out.at[:, 0:4, rows])
        put(held.at[:, pl.ds(8 * half + 4, 4)], out.at[:, 12:16, rows])
    put(held.at[:, 16], out.at[:, 4, 0:8])
    put(held.at[:, 17], out.at[:, 0, 8:16])
    for copy in copies:
        copy.wait()


def per_device(psi_coeff, potential, projectors, coupling, positions, species):
    f32, bf16 = jnp.float32, jnp.bfloat16
    consts = [jnp.asarray(table) for table in tables()]
    hbm = pl.BlockSpec(memory_space=pltpu.HBM)
    vmem = pl.BlockSpec(memory_space=pltpu.VMEM)
    columns = pl.pallas_call(
        kernel,
        out_shape=jax.ShapeDtypeStruct((2, 18, 8, N), f32),
        in_specs=[hbm] * 11,
        out_specs=vmem,
        scratch_shapes=[
            pltpu.VMEM((2, 9, 32, N), f32),
            pltpu.VMEM((2, 2, N, 128), f32),
            pltpu.VMEM((NSPEC, LPROJ, 9, 32, N), bf16),
            pltpu.VMEM((LPROJ, NSPEC, LPROJ), f32),
            pltpu.VMEM((3, ATOMS), f32),
            pltpu.VMEM((1, ATOMS), jnp.int32),
            pltpu.VMEM((2, 512, 512), bf16),
            pltpu.VMEM((2, 256, 1024), bf16),
            pltpu.VMEM((2, 1024, 256), bf16),
            pltpu.VMEM((4, 256, 256), bf16),
            pltpu.VMEM((2, 128, 512), f32),
            pltpu.VMEM((2, COLS, N), f32),
            pltpu.VMEM((NSPEC * LPROJ, COLS, N), f32),
            pltpu.VMEM((2, 2 * N, 2 * ATOMS), bf16),
            pltpu.VMEM((2, COLS, 2 * ATOMS), f32),
            pltpu.VMEM((2, 128, 512), f32),
            pltpu.VMEM((2, COLS, N), f32),
            pltpu.VMEM((2, 256, COLS), f32),
            pltpu.VMEM((2, 256, COLS), f32),
            pltpu.VMEM((2, 256, COLS), f32),
            pltpu.VMEM((2, 256, COLS), f32),
            pltpu.VMEM((2, 8, 128), f32),
            pltpu.VMEM((GX, 8, 128), f32),
            pltpu.VMEM((GY, 8, 128), f32),
            pltpu.SemaphoreType.DMA((14,)),
            pltpu.SemaphoreType.DMA((12,)),
            pltpu.SemaphoreType.REGULAR,
        ],
        compiler_params=pltpu.CompilerParams(
            collective_id=0, has_side_effects=True, vmem_limit_bytes=60 * 1024 * 1024
        ),
    )(
        psi_coeff,
        potential,
        projectors,
        jnp.transpose(coupling, (1, 0, 2)),
        positions,
        species.reshape(1, ATOMS),
        *consts,
    )
    return pl.pallas_call(
        place,
        out_shape=jax.ShapeDtypeStruct((2, 16, 32, N), f32),
        in_specs=[hbm],
        out_specs=hbm,
        scratch_shapes=[
            pltpu.VMEM((2, 18, 8, N), f32),
            pltpu.VMEM((7, 32, N), f32),
            pltpu.SemaphoreType.DMA,
            pltpu.SemaphoreType.DMA((16,)),
        ],
        compiler_params=pltpu.CompilerParams(vmem_limit_bytes=60 * 1024 * 1024),
    )(columns)


def solution(mesh):
    in_specs = (
        P("band", "gx", "gy", None),
        P(("gx", "gy"), None, None),
        P(None, None, "gx", "gy", None),
        P(),
        P(),
        P(),
    )
    out_specs = P("band", "gx", "gy", None)
    return jax.shard_map(
        per_device, mesh=mesh, in_specs=in_specs, out_specs=out_specs, check_vma=False
    )
```

```python
import functools
import math

import jax
import jax.numpy as jnp
import ml_dtypes
import numpy as np
from jax import lax
from jax.experimental import pallas as pl
from jax.experimental.pallas import tpu as pltpu
from jax.sharding import PartitionSpec as P

MESH = pl.DeviceIdType.MESH
N = 256
GX = 16
GY = 8
COLS = 128
RADIUS = 64
ATOMS = 64
NSPEC = 2
LPROJ = 3
TWO_PI = 2.0 * math.pi
ROWS_X = (0, 1, 2, 3, 12, 13, 14, 15)
HELD_X = (0, 1, 2, 3, 5, 6, 7, 8)
COL_Y = 71
COL_X = 72
COL_Z = 73


def column_offsets(col):
    a = col // 16
    b = col % 16
    a = a - 8 * (a >= 4)
    b = b - 16 * (b >= 8)
    a = np.where(col == COL_Y, 0, np.where(col == COL_X, 4, a))
    b = np.where(col == COL_Y, 8, np.where(col == COL_X, 0, b))
    return a, b


def two_parts(table):
    table = table.astype(np.float32)
    high = table.astype(ml_dtypes.bfloat16)
    low = (table - high.astype(np.float32)).astype(ml_dtypes.bfloat16)
    return np.stack([high, low])


@functools.lru_cache(maxsize=None)
def tables():
    t, g, y, c = np.meshgrid(
        np.arange(2), np.arange(GX), np.arange(GY), np.arange(2), indexing="ij"
    )
    z = (16 * g + 2 * y + t).reshape(-1, 1)
    c = c.reshape(-1, 1)
    angle = TWO_PI / N * (z * np.arange(N)[None, :] % N)
    cos, sin = np.cos(angle) / 16, np.sin(angle) / 16
    tz = np.concatenate(
        [np.where(c == 0, cos, sin), np.where(c == 0, -sin, cos)], axis=1
    )
    a, b = column_offsets(np.arange(COLS))
    x0 = np.repeat(np.arange(16), 32)[None, :]
    y0 = np.tile(np.arange(32), 16)[None, :]
    angle = TWO_PI * ((2 * a[:, None] * x0 + b[:, None] * y0) % 32) / 32
    cos, sin = np.cos(angle) / 16, np.sin(angle) / 16
    t1 = np.block([[cos, sin], [-sin, cos]])
    gy = np.repeat(np.arange(GY), GX)[:, None]
    gx = np.tile(np.arange(GX), GY)[:, None]
    angle = TWO_PI * ((gx * x0 + gy * y0) % N) / N
    t2 = np.stack([np.cos(angle), np.sin(angle)]).astype(np.float32)
    y1, x1 = gy, gx
    angle = TWO_PI * ((gx.T * x1 + 2 * gy.T * y1) % 16) / 16
    cos, sin = np.cos(angle) / 16, np.sin(angle) / 16
    e = np.block([[cos, -sin], [sin, cos]])
    return (
        two_parts(tz),
        two_parts(t1),
        two_parts(t1.T),
        np.concatenate([two_parts(e), two_parts(e.T)]),
        t2,
    )


def split(value):
    high = value.astype(jnp.bfloat16)
    return high, (value - high.astype(jnp.float32)).astype(jnp.bfloat16)


def product(left, right, dims=((1,), (0,))):
    def one(first, second):
        return lax.dot_general(
            first, second, (dims, ((), ())), preferred_element_type=jnp.float32
        )

    return one(left[0], right[0]) + (one(left[0], right[1]) + one(left[1], right[0]))


def cos_turns(turns):
    r = (turns - jnp.floor(turns + 0.5)) * math.pi
    r2 = r * r
    s = -1.0 / 39916800.0
    for denom in (362880.0, -5040.0, 120.0, -6.0, 1.0):
        s = s * r2 + 1.0 / denom
    s = s * r
    return 1.0 - 2.0 * s * s


def iota(shape, axis):
    return lax.broadcasted_iota(jnp.int32, shape, axis)


def column_freqs(gx, gy, shape):
    col = iota(shape, 0)
    a = lax.shift_right_logical(col, 4)
    b = col & 15
    a = jnp.where(a >= 4, a - 8, a)
    b = jnp.where(b >= 8, b - 16, b)
    a = jnp.where(col == COL_Y, 0, jnp.where(col == COL_X, 4, a))
    b = jnp.where(col == COL_Y, 8, jnp.where(col == COL_X, 0, b))
    return gx + GX * a, gy + GY * b


def fractional(product_):
    return product_ - jnp.floor(product_)


def inner(value):
    row, lane = iota((COLS, COLS), 0), iota((COLS, COLS), 1)
    both = jnp.where(lane < RADIUS, value[:, :COLS], value[:, COLS:])
    extra = jnp.broadcast_to(value[0:1, RADIUS : RADIUS + 1], (COLS, COLS))
    return jnp.where((row == COL_Z) & (lane == 0), extra, both)


def pick_columns(held):
    tiles = []
    for place, i in enumerate(HELD_X):
        row = held(i)
        first, second = row[0:8], row[24:32]
        if place == 4:
            sub = iota((8, N), 0)
            other = jnp.broadcast_to(held(0)[8:9], (8, N))
            first = jnp.where(sub == 7, other, first)
            other = jnp.broadcast_to(held(4)[0:1], (8, N))
            second = jnp.where(sub == 0, other, second)
        tiles += [first, second]
    return jnp.concatenate(tiles, axis=0)


def kernel(
    psi_h, pot_h, proj_h, coup_h, pos_h, spec_h, tz_h, t1_h, t1t_h, e_h, t2_h,
    out,
    psi, pot, proj, coup, pos, spec, tz, t1, t1t, e, t2,
    xs, pf, pz, pxy, vt, nl,
    zs, r2, s3, r4, ar0, ar1, ar2,
    load_sem, sems, ready,
):
    gx = lax.axis_index("gx")
    gy = lax.axis_index("gy")
    loads = []
    pairs = [
        (psi_h.at[:, 0:5], psi.at[:, 0:5]),
        (psi_h.at[:, 12:16], psi.at[:, 5:9]),
        (tz_h, tz),
        (proj_h.at[:, :, 0:5], proj.at[:, :, 0:5]),
        (proj_h.at[:, :, 12:16], proj.at[:, :, 5:9]),
        (pot_h.at[:, :, 0:128], pot.at[0]),
        (pot_h.at[:, :, 128:256], pot.at[1]),
        (t1_h, t1),
        (t2_h, t2),
        (e_h, e),
        (t1t_h, t1t),
        (pos_h, pos),
        (spec_h, spec),
        (coup_h, coup),
    ]
    for i, (src, dst) in enumerate(pairs):
        loads.append(pltpu.make_async_copy(src, dst, load_sem.at[i]))
    for load in loads[:3]:
        load.start()
    barrier = pltpu.get_barrier_semaphore()
    for d in range(1, GX):
        pl.semaphore_signal(
            barrier, inc=1, device_id={"gx": lax.rem(gx + d, GX)}, device_id_type=MESH
        )
    for d in range(1, GY):
        pl.semaphore_signal(
            barrier, inc=1, device_id={"gy": lax.rem(gy + d, GY)}, device_id_type=MESH
        )
    for load in loads[3:]:
        load.start()

    def exchange(axis, me, count, slot, source, target, block, landing):
        send_sem, recv_sem = sems.at[2 * slot], sems.at[2 * slot + 1]

        def post(d):
            peer = lax.rem(me + d, count)
            pltpu.make_async_remote_copy(
                src_ref=source(peer),
                dst_ref=target(me),
                send_sem=send_sem,
                recv_sem=recv_sem,
                device_id={axis: peer},
                device_id_type=MESH,
            ).start()

        for k in range(1, count):
            d = count // 2 - k // 2 if k % 2 == 1 else count // 2 + k // 2
            post(d)
        pltpu.make_async_copy(source(me), target(me), recv_sem).start()

        def sent():
            pltpu.make_async_copy(block, block, send_sem).wait()

        def landed():
            pltpu.make_async_copy(landing, landing, recv_sem).wait()

        return sent, landed

    def over_x(*args):
        return exchange("gx", gx, GX, *args)

    def over_y(*args):
        return exchange("gy", gy, GY, *args)

    by_x = [lax.rem(gx + d, GX) for d in range(GX)]
    by_y = [lax.rem(gy + d, GY) for d in range(GY)]

    def exchange_all(slot, source, target, source_at, target_at):
        send_sem, recv_sem = sems.at[2 * slot], sems.at[2 * slot + 1]
        mine = target.at[pl.ds(target_at(gx, gy), 2), :]

        def post(px, py):
            pltpu.make_async_remote_copy(
                src_ref=source.at[pl.ds(source_at(px, py), 2), :],
                dst_ref=mine,
                send_sem=send_sem,
                recv_sem=recv_sem,
                device_id={"gx": px, "gy": py},
                device_id_type=MESH,
            ).start()

        def step(j):
            @pl.loop(0, GY)
            def _(d):
                py = lax.rem(gy + d, GY)
                post(by_x[8 - j], py)
                if j > 0:
                    post(by_x[8 + j], py)

        def last():
            for py in by_y[1:]:
                post(gx, py)
            pltpu.make_async_copy(
                source.at[pl.ds(source_at(gx, gy), 2), :], mine, recv_sem
            ).start()

        steps = [functools.partial(step, j) for j in range(8)] + [last]

        def sent():
            block = source.at[pl.ds(0, 254), :]
            pltpu.make_async_copy(block, block, send_sem).wait()

        def landed():
            pltpu.make_async_copy(target, target, recv_sem).wait()

        return steps, sent, landed

    def by_gx(px, py):
        return (px * GY + py) * 2

    def by_gy(px, py):
        return (py * GX + px) * 2

    kx, ky = column_freqs(gx, gy, (COLS, N))
    lane = iota((COLS, N), 1)
    kz = jnp.where(lane < N // 2, lane, lane - N)
    squared = kx * kx + ky * ky + kz * kz
    inside = squared <= RADIUS * RADIUS
    kinetic = squared.astype(jnp.float32) * (1.0 / (RADIUS * RADIUS))
    loads[0].wait()
    loads[1].wait()
    for c in range(2):
        xs[c] = jnp.where(inside, pick_columns(lambda i: psi[c, i]), 0.0)
    x_parts = split(jnp.concatenate([xs[0], xs[1]], axis=1))
    loads[2].wait()

    def tz_parts(t):
        rows = pl.ds(256 * t, 256)
        return tz[0, rows, :], tz[1, rows, :]

    few_x, few_y = pl.ds(0, GX - 1), pl.ds(0, GY - 1)

    def lines(t):
        zs[t] = product(tz_parts(t), x_parts, ((1,), (1,)))

    def scatter(t):
        return exchange_all(t, zs.at[t], r2.at[t], by_gx, by_gy)

    lines(0)
    pl.semaphore_wait(barrier, GX + GY - 2)
    for py in by_y[1:]:
        pl.semaphore_signal(ready, inc=1, device_id={"gy": py}, device_id_type=MESH)
    lines(1)
    pl.semaphore_wait(ready, GY - 1)
    steps, sent1, landed1 = zip(scatter(0), scatter(1))
    queue = [*steps[0], *steps[1]]

    def proceed(count=1):
        for _ in range(min(count, len(queue))):
            queue.pop(0)()

    proceed(3)
    for c in range(2):
        for row in range(16):
            if row in ROWS_X:
                out[c, row, 8:24, :] = jnp.zeros((16, N), jnp.float32)
            else:
                out[c, row] = jnp.zeros((32, N), jnp.float32)

    loads[11].wait()
    loads[12].wait()
    loads[13].wait()
    atoms2 = jnp.concatenate([pos[...], pos[...]], axis=1)
    half = iota((1, 2 * ATOMS), 1) >= ATOMS
    quarter = jnp.where(half, 0.25, 0.0)
    row = iota((COLS, 2 * ATOMS), 0)
    kz_rows = jnp.where(row < RADIUS, row, row - 2 * RADIUS).astype(jnp.float32)
    turns_z = fractional(kz_rows * atoms2[2:3])
    pz_f32 = jnp.concatenate(
        [cos_turns(turns_z - quarter), cos_turns(turns_z + (0.25 - quarter))], axis=0
    )
    pz[0], pz[1] = split(pz_f32)
    proceed()
    kx_col, ky_col = column_freqs(gx, gy, (COLS, 2 * ATOMS))
    turns_xy = fractional(kx_col.astype(jnp.float32) * atoms2[0:1]) + fractional(
        ky_col.astype(jnp.float32) * atoms2[1:2]
    )
    turns_xy = jnp.where(row == COL_Z, fractional(RADIUS * atoms2[2:3]), turns_xy)
    pxy[0] = cos_turns(turns_xy)
    pxy[1] = cos_turns(turns_xy + jnp.where(half, -0.25, 0.25))
    proceed()

    loads[3].wait()
    loads[4].wait()
    pz_parts = (pz[0], pz[1])
    inner_re, inner_im = inner(xs[0]), inner(xs[1])
    sums = []
    for s in range(NSPEC):
        weighted = []
        for q in range(LPROJ):
            factor = inner(pick_columns(lambda i: proj[s, q, i].astype(jnp.float32)))
            pf[s * LPROJ + q] = factor
            weighted.append(jnp.concatenate([factor * inner_re, factor * inner_im], axis=1))
            proceed(3)
        along_z = product(split(jnp.concatenate(weighted, axis=0)), pz_parts)
        for q in range(LPROJ):
            part = along_z[COLS * q : COLS * (q + 1)]
            along = part * pxy[0] + pltpu.roll(part, ATOMS, 1) * pxy[1]
            sums.append(jnp.sum(along, axis=0, keepdims=True))
    species = jnp.concatenate([spec[...], spec[...]], axis=1)
    norm = 4.0 / math.sqrt(N * N * N)
    sub = iota((8, 2 * ATOMS), 0)
    part = jnp.zeros((8, 2 * ATOMS), jnp.float32)
    for q in range(LPROJ):
        chosen = jnp.where(species == 0, sums[q], sums[LPROJ + q]) * norm
        part = jnp.where(sub == q, chosen, part)
    ar0[0] = part
    sent_a1, landed_a1 = over_x(
        4, lambda p: ar0.at[0], lambda m: ar1.at[m], ar1.at[few_x], ar1
    )

    loads[5].wait()
    loads[6].wait()
    lane16 = iota((16, 128), 1)
    for t in range(2):
        for block in range(4):
            for hy in range(2):
                strips = [
                    pot[hy, t, pl.ds(4 * block + j, 16, stride=16), :] for j in range(4)
                ]
                for r in range(4):
                    tile = None
                    for j in range(4):
                        shift = (32 * (j - r)) % 128
                        moved = strips[j] if shift == 0 else pltpu.roll(strips[j], shift, 1)
                        tile = moved if tile is None else jnp.where(lane16 >= 32 * j, moved, tile)
                    y1 = 4 * hy + r
                    vt[t, pl.ds(16 * y1, 16), pl.ds(128 * block, 128)] = tile
        proceed(1)

    def plane(t):
        landed1[t]()
        values = jnp.concatenate(
            [r2[t, pl.ds(0, COLS, stride=2), :], r2[t, pl.ds(1, COLS, stride=2), :]], axis=1
        )
        lanes = product(split(values), (t1[0], t1[1]))
        proceed(2)
        lanes_re, lanes_im = lanes[:, :512], lanes[:, 512:]
        cos, sin = t2[0], t2[1]
        turned = jnp.concatenate(
            [lanes_re * cos - lanes_im * sin, lanes_re * sin + lanes_im * cos], axis=0
        )
        space = product((e[0], e[1]), split(turned))
        proceed(2)
        field = jnp.concatenate([space[:128] * vt[t], space[128:] * vt[t]], axis=0)
        rows = product((e[2], e[3]), split(field))
        proceed(2)
        rows_re, rows_im = rows[:128], rows[128:]
        turned = jnp.concatenate(
            [rows_re * cos + rows_im * sin, rows_im * cos - rows_re * sin], axis=1
        )
        back = product(split(turned), (t1t[0], t1t[1]))
        s3[t, pl.ds(0, COLS, stride=2), :] = back[:, :128]
        s3[t, pl.ds(1, COLS, stride=2), :] = back[:, 128:]

    def gather(t):
        return exchange_all(2 + t, s3.at[t], r4.at[t], by_gy, by_gx)

    steps4, sent4, landed4 = zip(gather(0), gather(1))
    for i in range(7, 11):
        loads[i].wait()
    proceed(9)
    plane(0)
    proceed(len(queue))
    queue += steps4[0]
    proceed(9)
    landed_a1()
    total = ar1[0]
    for g in range(1, GX):
        total += ar1[g]
    ar0[1] = total
    sent_a2, landed_a2 = over_y(
        5, lambda p: ar0.at[1], lambda m: ar2.at[m], ar2.at[few_y], ar2
    )
    proceed(9)
    plane(1)
    proceed(len(queue))
    queue += steps4[1]
    proceed(9)

    landed_a2()
    total = ar2[0]
    for g in range(1, GY):
        total += ar2[g]
    spread = []
    for s in range(NSPEC):
        for q in range(LPROJ):
            weight = coup[q, s : s + 1, 0:1] * total[0:1]
            for m in range(1, LPROJ):
                weight += coup[q, s : s + 1, m : m + 1] * total[m : m + 1]
            weight = weight * (1.0 / math.sqrt(ATOMS * LPROJ))
            spread.append(jnp.where(species == s, weight, 0.0))
    nonloc = None
    for s in range(NSPEC):
        at_columns = []
        for weight in spread[LPROJ * s : LPROJ * (s + 1)]:
            around = pltpu.roll(jnp.broadcast_to(weight, (8, 2 * ATOMS)), ATOMS, 1)[0:1]
            at_columns.append(pxy[0] * weight - pxy[1] * around)
        at_columns = jnp.concatenate(at_columns, axis=0)
        spread_z = product(split(at_columns), pz_parts, ((1,), (1,)))
        for q in range(LPROJ):
            factor = pf[s * LPROJ + q]
            part = spread_z[COLS * q : COLS * (q + 1)]
            term = jnp.concatenate([factor * part[:, :COLS], factor * part[:, COLS:]], axis=1)
            nonloc = term if nonloc is None else nonloc + term
        proceed(1)
    row, lane = iota((COLS, COLS), 0), iota((COLS, COLS), 1)
    for c in range(2):
        part = nonloc[:, c * COLS : (c + 1) * COLS]
        extra = jnp.broadcast_to(part[COL_Z : COL_Z + 1, 0:1], (COLS, COLS))
        low = jnp.where((row == 0) & (lane == RADIUS), extra, part)
        nl[c] = jnp.concatenate([low, part], axis=1) + kinetic * xs[c]

    proceed(len(queue))
    recip = None
    for t in range(2):
        landed4[t]()
        term = product(split(jnp.transpose(r4[t])), tz_parts(t))
        recip = term if recip is None else recip + term
    for c in range(2):
        value = jnp.where(inside, nl[c] + recip[:, c * N : (c + 1) * N], 0.0)
        tiles = [value[8 * k : 8 * k + 8] for k in range(16)]
        sub = iota((8, N), 0)
        row = jnp.broadcast_to(value[COL_X : COL_X + 1], (8, N))
        out[c, 4, 0:8, :] = jnp.where(sub == 0, row, 0.0)
        row = jnp.broadcast_to(value[COL_Y : COL_Y + 1], (8, N))
        out[c, 0, 8:16, :] = jnp.where(sub == 0, row, 0.0)
        tiles[8] = jnp.where(sub == COL_Y % 8, 0.0, tiles[8])
        tiles[9] = jnp.where(sub == COL_X % 8, 0.0, tiles[9])
        for k, row in enumerate(ROWS_X):
            out[c, row, 0:8, :] = tiles[2 * k]
            out[c, row, 24:32, :] = tiles[2 * k + 1]
    for sent in (*sent1, *sent4, sent_a1, sent_a2):
        sent()


def per_device(psi_coeff, potential, projectors, coupling, positions, species):
    f32, bf16 = jnp.float32, jnp.bfloat16
    consts = [jnp.asarray(table) for table in tables()]
    hbm = pl.BlockSpec(memory_space=pltpu.HBM)
    vmem = pl.BlockSpec(memory_space=pltpu.VMEM)
    return pl.pallas_call(
        kernel,
        out_shape=pltpu.VMEM((2, 16, 32, N), f32),
        in_specs=[hbm] * 11,
        out_specs=vmem,
        scratch_shapes=[
            pltpu.VMEM((2, 9, 32, N), f32),
            pltpu.VMEM((2, 2, N, 128), f32),
            pltpu.VMEM((NSPEC, LPROJ, 9, 32, N), bf16),
            pltpu.VMEM((LPROJ, NSPEC, LPROJ), f32),
            pltpu.VMEM((3, ATOMS), f32),
            pltpu.VMEM((1, ATOMS), jnp.int32),
            pltpu.VMEM((2, 512, 512), bf16),
            pltpu.VMEM((2, 256, 1024), bf16),
            pltpu.VMEM((2, 1024, 256), bf16),
            pltpu.VMEM((4, 256, 256), bf16),
            pltpu.VMEM((2, 128, 512), f32),
            pltpu.VMEM((2, COLS, N), f32),
            pltpu.VMEM((NSPEC * LPROJ, COLS, COLS), f32),
            pltpu.VMEM((2, 2 * COLS, 2 * ATOMS), bf16),
            pltpu.VMEM((2, COLS, 2 * ATOMS), f32),
            pltpu.VMEM((2, 128, 512), f32),
            pltpu.VMEM((2, COLS, N), f32),
            pltpu.VMEM((2, 256, COLS), f32),
            pltpu.VMEM((2, 256, COLS), f32),
            pltpu.VMEM((2, 256, COLS), f32),
            pltpu.VMEM((2, 256, COLS), f32),
            pltpu.VMEM((2, 8, 128), f32),
            pltpu.VMEM((GX, 8, 128), f32),
            pltpu.VMEM((GY, 8, 128), f32),
            pltpu.SemaphoreType.DMA((14,)),
            pltpu.SemaphoreType.DMA((12,)),
            pltpu.SemaphoreType.REGULAR,
        ],
        compiler_params=pltpu.CompilerParams(
            collective_id=0, has_side_effects=True, vmem_limit_bytes=57 * 1024 * 1024
        ),
    )(
        psi_coeff,
        potential,
        projectors,
        jnp.transpose(coupling, (1, 0, 2)),
        positions,
        species.reshape(1, ATOMS),
        *consts,
    )


def solution(mesh):
    in_specs = (
        P("band", "gx", "gy", None),
        P(("gx", "gy"), None, None),
        P(None, None, "gx", "gy", None),
        P(),
        P(),
        P(),
    )
    out_specs = P("band", "gx", "gy", None)
    return jax.shard_map(
        per_device, mesh=mesh, in_specs=in_specs, out_specs=out_specs, check_vma=False
    )
```

```python
import functools
import math

import jax
import jax.numpy as jnp
import ml_dtypes
import numpy as np
from jax import lax
from jax.experimental import pallas as pl
from jax.experimental.pallas import tpu as pltpu
from jax.sharding import PartitionSpec as P

MESH = pl.DeviceIdType.MESH
N = 256
GX = 16
GY = 8
COLS = 128
RADIUS = 64
ATOMS = 64
NSPEC = 2
LPROJ = 3
TWO_PI = 2.0 * math.pi
ROWS_X = (0, 1, 2, 3, 12, 13, 14, 15)
HELD_X = (0, 1, 2, 3, 5, 6, 7, 8)
COL_Y = 71
COL_X = 72
COL_Z = 73


def column_offsets(col):
    a = col // 16
    b = col % 16
    a = a - 8 * (a >= 4)
    b = b - 16 * (b >= 8)
    a = np.where(col == COL_Y, 0, np.where(col == COL_X, 4, a))
    b = np.where(col == COL_Y, 8, np.where(col == COL_X, 0, b))
    return a, b


def two_parts(table):
    table = table.astype(np.float32)
    high = table.astype(ml_dtypes.bfloat16)
    low = (table - high.astype(np.float32)).astype(ml_dtypes.bfloat16)
    return np.stack([high, low])


@functools.lru_cache(maxsize=None)
def tables():
    t, g, y, c = np.meshgrid(
        np.arange(2), np.arange(GX), np.arange(GY), np.arange(2), indexing="ij"
    )
    z = (16 * g + 2 * y + t).reshape(-1, 1)
    c = c.reshape(-1, 1)
    angle = TWO_PI / N * (z * np.arange(N)[None, :] % N)
    cos, sin = np.cos(angle) / 16, np.sin(angle) / 16
    tz = np.concatenate(
        [np.where(c == 0, cos, sin), np.where(c == 0, -sin, cos)], axis=1
    )
    a, b = column_offsets(np.arange(COLS))
    x0 = np.repeat(np.arange(16), 32)[None, :]
    y0 = np.tile(np.arange(32), 16)[None, :]
    angle = TWO_PI * ((2 * a[:, None] * x0 + b[:, None] * y0) % 32) / 32
    cos, sin = np.cos(angle) / 16, np.sin(angle) / 16
    t1 = np.block([[cos, sin], [-sin, cos]])
    gy = np.repeat(np.arange(GY), GX)[:, None]
    gx = np.tile(np.arange(GX), GY)[:, None]
    angle = TWO_PI * ((gx * x0 + gy * y0) % N) / N
    t2 = np.stack([np.cos(angle), np.sin(angle)]).astype(np.float32)
    y1, x1 = gy, gx
    angle = TWO_PI * ((gx.T * x1 + 2 * gy.T * y1) % 16) / 16
    cos, sin = np.cos(angle) / 16, np.sin(angle) / 16
    e = np.block([[cos, -sin], [sin, cos]])
    return (
        two_parts(tz),
        two_parts(t1),
        two_parts(t1.T),
        np.concatenate([two_parts(e), two_parts(e.T)]),
        t2,
    )


def split(value):
    high = value.astype(jnp.bfloat16)
    return high, (value - high.astype(jnp.float32)).astype(jnp.bfloat16)


def product(left, right, dims=((1,), (0,))):
    def one(first, second):
        return lax.dot_general(
            first, second, (dims, ((), ())), preferred_element_type=jnp.float32
        )

    return one(left[0], right[0]) + (one(left[0], right[1]) + one(left[1], right[0]))


def cos_turns(turns):
    r = (turns - jnp.floor(turns + 0.5)) * math.pi
    r2 = r * r
    s = -1.0 / 39916800.0
    for denom in (362880.0, -5040.0, 120.0, -6.0, 1.0):
        s = s * r2 + 1.0 / denom
    s = s * r
    return 1.0 - 2.0 * s * s


def iota(shape, axis):
    return lax.broadcasted_iota(jnp.int32, shape, axis)


def column_freqs(gx, gy, shape):
    col = iota(shape, 0)
    a = lax.shift_right_logical(col, 4)
    b = col & 15
    a = jnp.where(a >= 4, a - 8, a)
    b = jnp.where(b >= 8, b - 16, b)
    a = jnp.where(col == COL_Y, 0, jnp.where(col == COL_X, 4, a))
    b = jnp.where(col == COL_Y, 8, jnp.where(col == COL_X, 0, b))
    return gx + GX * a, gy + GY * b


def fractional(product_):
    return product_ - jnp.floor(product_)


def inner(value):
    row, lane = iota((COLS, COLS), 0), iota((COLS, COLS), 1)
    both = jnp.where(lane < RADIUS, value[:, :COLS], value[:, COLS:])
    extra = jnp.broadcast_to(value[0:1, RADIUS : RADIUS + 1], (COLS, COLS))
    return jnp.where((row == COL_Z) & (lane == 0), extra, both)


def pick_columns(held):
    tiles = []
    for place, i in enumerate(HELD_X):
        row = held(i)
        first, second = row[0:8], row[24:32]
        if place == 4:
            sub = iota((8, N), 0)
            other = jnp.broadcast_to(held(0)[8:9], (8, N))
            first = jnp.where(sub == 7, other, first)
            other = jnp.broadcast_to(held(4)[0:1], (8, N))
            second = jnp.where(sub == 0, other, second)
        tiles += [first, second]
    return jnp.concatenate(tiles, axis=0)


def kernel(
    psi_h, pot_h, proj_h, coup_h, pos_h, spec_h, tz_h, t1_h, t1t_h, e_h, t2_h,
    out,
    psi, pot, proj, coup, pos, spec, tz, t1, t1t, e, t2,
    xs, pf, pz, pxy, vt, nl,
    zs, r2, s3, r4, ar0, ar1, ar2,
    load_sem, sems,
):
    gx = lax.axis_index("gx")
    gy = lax.axis_index("gy")
    loads = []
    pairs = [
        (psi_h.at[:, 0:5], psi.at[:, 0:5]),
        (psi_h.at[:, 12:16], psi.at[:, 5:9]),
        (tz_h, tz),
        (proj_h.at[:, :, 0:5], proj.at[:, :, 0:5]),
        (proj_h.at[:, :, 12:16], proj.at[:, :, 5:9]),
        (pot_h.at[:, :, 0:128], pot.at[0]),
        (pot_h.at[:, :, 128:256], pot.at[1]),
        (t1_h, t1),
        (t2_h, t2),
        (e_h, e),
        (t1t_h, t1t),
        (pos_h, pos),
        (spec_h, spec),
        (coup_h, coup),
    ]
    for i, (src, dst) in enumerate(pairs):
        loads.append(pltpu.make_async_copy(src, dst, load_sem.at[i]))
    for load in loads[:3]:
        load.start()
    barrier = pltpu.get_barrier_semaphore()
    by_x = [lax.rem(gx + d, GX) for d in range(GX)]
    by_y = [lax.rem(gy + d, GY) for d in range(GY)]

    def greet(px, py):
        pl.semaphore_signal(
            barrier, inc=1, device_id={"gx": px, "gy": py}, device_id_type=MESH
        )

    def greet_rows(j):
        @pl.loop(0, GY)
        def _(d):
            py = lax.rem(gy + d, GY)
            greet(by_x[8 - j], py)
            if j > 0:
                greet(by_x[8 + j], py)

    for j in range(8):
        greet_rows(j)
    for py in by_y[1:]:
        greet(gx, py)
    for load in loads[3:]:
        load.start()

    def exchange(axis, me, count, slot, source, target, block, landing):
        send_sem, recv_sem = sems.at[2 * slot], sems.at[2 * slot + 1]

        def post(d):
            peer = lax.rem(me + d, count)
            pltpu.make_async_remote_copy(
                src_ref=source(peer),
                dst_ref=target(me),
                send_sem=send_sem,
                recv_sem=recv_sem,
                device_id={axis: peer},
                device_id_type=MESH,
            ).start()

        for k in range(1, count):
            d = count // 2 - k // 2 if k % 2 == 1 else count // 2 + k // 2
            post(d)
        pltpu.make_async_copy(source(me), target(me), recv_sem).start()

        def sent():
            pltpu.make_async_copy(block, block, send_sem).wait()

        def landed():
            pltpu.make_async_copy(landing, landing, recv_sem).wait()

        return sent, landed

    def over_x(*args):
        return exchange("gx", gx, GX, *args)

    def over_y(*args):
        return exchange("gy", gy, GY, *args)

    def exchange_all(slot, source, target, source_at, target_at):
        send_sem, recv_sem = sems.at[2 * slot], sems.at[2 * slot + 1]
        mine = target.at[pl.ds(target_at(gx, gy), 2), :]

        def post(px, py):
            pltpu.make_async_remote_copy(
                src_ref=source.at[pl.ds(source_at(px, py), 2), :],
                dst_ref=mine,
                send_sem=send_sem,
                recv_sem=recv_sem,
                device_id={"gx": px, "gy": py},
                device_id_type=MESH,
            ).start()

        def step(j):
            @pl.loop(0, GY)
            def _(d):
                py = lax.rem(gy + d, GY)
                post(by_x[8 - j], py)
                if j > 0:
                    post(by_x[8 + j], py)

        def last():
            for py in by_y[1:]:
                post(gx, py)
            pltpu.make_async_copy(
                source.at[pl.ds(source_at(gx, gy), 2), :], mine, recv_sem
            ).start()

        steps = [functools.partial(step, j) for j in range(8)] + [last]

        def sent():
            block = source.at[pl.ds(0, 254), :]
            pltpu.make_async_copy(block, block, send_sem).wait()

        def landed():
            pltpu.make_async_copy(target, target, recv_sem).wait()

        return steps, sent, landed

    def by_gx(px, py):
        return (px * GY + py) * 2

    def by_gy(px, py):
        return (py * GX + px) * 2

    kx, ky = column_freqs(gx, gy, (COLS, N))
    lane = iota((COLS, N), 1)
    kz = jnp.where(lane < N // 2, lane, lane - N)
    squared = kx * kx + ky * ky + kz * kz
    inside = squared <= RADIUS * RADIUS
    kinetic = squared.astype(jnp.float32) * (1.0 / (RADIUS * RADIUS))
    loads[0].wait()
    loads[1].wait()
    for c in range(2):
        xs[c] = jnp.where(inside, pick_columns(lambda i: psi[c, i]), 0.0)
    x_parts = split(jnp.concatenate([xs[0], xs[1]], axis=1))
    loads[2].wait()

    def tz_parts(t):
        rows = pl.ds(256 * t, 256)
        return tz[0, rows, :], tz[1, rows, :]

    def lines(t):
        zs[t] = product(tz_parts(t), x_parts, ((1,), (1,)))

    def scatter(t):
        return exchange_all(t, zs.at[t], r2.at[t], by_gx, by_gy)

    lines(0)
    lines(1)
    pl.semaphore_wait(barrier, GX * GY - 1)
    steps, sent1, landed1 = zip(scatter(0), scatter(1))
    queue = [*steps[0], *steps[1]]

    def proceed(count=1):
        for _ in range(min(count, len(queue))):
            queue.pop(0)()

    proceed(3)
    for c in range(2):
        for row in range(16):
            if row in ROWS_X:
                out[c, row, 8:24, :] = jnp.zeros((16, N), jnp.float32)
            else:
                out[c, row] = jnp.zeros((32, N), jnp.float32)

    loads[11].wait()
    loads[12].wait()
    loads[13].wait()
    atoms2 = jnp.concatenate([pos[...], pos[...]], axis=1)
    half = iota((1, 2 * ATOMS), 1) >= ATOMS
    quarter = jnp.where(half, 0.25, 0.0)
    row = iota((COLS, 2 * ATOMS), 0)
    kz_rows = jnp.where(row < RADIUS, row, row - 2 * RADIUS).astype(jnp.float32)
    turns_z = fractional(kz_rows * atoms2[2:3])
    pz_f32 = jnp.concatenate(
        [cos_turns(turns_z - quarter), cos_turns(turns_z + (0.25 - quarter))], axis=0
    )
    pz[0], pz[1] = split(pz_f32)
    proceed()
    kx_col, ky_col = column_freqs(gx, gy, (COLS, 2 * ATOMS))
    turns_xy = fractional(kx_col.astype(jnp.float32) * atoms2[0:1]) + fractional(
        ky_col.astype(jnp.float32) * atoms2[1:2]
    )
    turns_xy = jnp.where(row == COL_Z, fractional(RADIUS * atoms2[2:3]), turns_xy)
    pxy[0] = cos_turns(turns_xy)
    pxy[1] = cos_turns(turns_xy + jnp.where(half, -0.25, 0.25))
    proceed()

    loads[3].wait()
    loads[4].wait()
    pz_parts = (pz[0], pz[1])
    inner_re, inner_im = inner(xs[0]), inner(xs[1])
    sums = []
    for s in range(NSPEC):
        weighted = []
        for q in range(LPROJ):
            factor = inner(pick_columns(lambda i: proj[s, q, i].astype(jnp.float32)))
            pf[s * LPROJ + q] = factor
            weighted.append(jnp.concatenate([factor * inner_re, factor * inner_im], axis=1))
            proceed(3)
        along_z = product(split(jnp.concatenate(weighted, axis=0)), pz_parts)
        for q in range(LPROJ):
            part = along_z[COLS * q : COLS * (q + 1)]
            along = part * pxy[0] + pltpu.roll(part, ATOMS, 1) * pxy[1]
            sums.append(jnp.sum(along, axis=0, keepdims=True))
    species = jnp.concatenate([spec[...], spec[...]], axis=1)
    norm = 4.0 / math.sqrt(N * N * N)
    for q in range(LPROJ):
        ar0[0, q : q + 1, :] = jnp.where(species == 0, sums[q], sums[LPROJ + q]) * norm
    sent_a1, landed_a1 = over_x(
        4, lambda p: ar0.at[0], lambda m: ar1.at[pl.ds(LPROJ * m, LPROJ), :],
        ar1.at[pl.ds(0, LPROJ * (GX - 1)), :], ar1,
    )

    loads[5].wait()
    loads[6].wait()
    lane16 = iota((16, 128), 1)
    for t in range(2):
        for block in range(4):
            for hy in range(2):
                strips = [
                    pot[hy, t, pl.ds(4 * block + j, 16, stride=16), :] for j in range(4)
                ]
                for r in range(4):
                    tile = None
                    for j in range(4):
                        shift = (32 * (j - r)) % 128
                        moved = strips[j] if shift == 0 else pltpu.roll(strips[j], shift, 1)
                        tile = moved if tile is None else jnp.where(lane16 >= 32 * j, moved, tile)
                    y1 = 4 * hy + r
                    vt[t, pl.ds(16 * y1, 16), pl.ds(128 * block, 128)] = tile
        proceed(1)

    def plane(t):
        landed1[t]()
        values = jnp.concatenate(
            [r2[t, pl.ds(0, COLS, stride=2), :], r2[t, pl.ds(1, COLS, stride=2), :]], axis=1
        )
        lanes = product(split(values), (t1[0], t1[1]))
        proceed(2)
        lanes_re, lanes_im = lanes[:, :512], lanes[:, 512:]
        cos, sin = t2[0], t2[1]
        turned = jnp.concatenate(
            [lanes_re * cos - lanes_im * sin, lanes_re * sin + lanes_im * cos], axis=0
        )
        space = product((e[0], e[1]), split(turned))
        proceed(2)
        field = jnp.concatenate([space[:128] * vt[t], space[128:] * vt[t]], axis=0)
        rows = product((e[2], e[3]), split(field))
        proceed(2)
        rows_re, rows_im = rows[:128], rows[128:]
        turned = jnp.concatenate(
            [rows_re * cos + rows_im * sin, rows_im * cos - rows_re * sin], axis=1
        )
        back = product(split(turned), (t1t[0], t1t[1]))
        s3[t, pl.ds(0, COLS, stride=2), :] = back[:, :128]
        s3[t, pl.ds(1, COLS, stride=2), :] = back[:, 128:]

    def gather(t):
        return exchange_all(2 + t, s3.at[t], r4.at[t], by_gy, by_gx)

    steps4, sent4, landed4 = zip(gather(0), gather(1))
    for i in range(7, 11):
        loads[i].wait()
    proceed(9)
    plane(0)
    proceed(len(queue))
    queue += steps4[0]
    proceed(9)
    landed_a1()
    total = ar1[0:LPROJ, :]
    for g in range(1, GX):
        total += ar1[LPROJ * g : LPROJ * (g + 1), :]
    ar0[1] = total
    sent_a2, landed_a2 = over_y(
        5, lambda p: ar0.at[1], lambda m: ar2.at[pl.ds(LPROJ * m, LPROJ), :],
        ar2.at[pl.ds(0, LPROJ * (GY - 1)), :], ar2,
    )
    proceed(9)
    plane(1)
    proceed(len(queue))
    queue += steps4[1]
    proceed(9)

    landed_a2()
    total = ar2[0:LPROJ, :]
    for g in range(1, GY):
        total += ar2[LPROJ * g : LPROJ * (g + 1), :]
    spread = []
    for s in range(NSPEC):
        for q in range(LPROJ):
            weight = coup[q, s : s + 1, 0:1] * total[0:1]
            for m in range(1, LPROJ):
                weight += coup[q, s : s + 1, m : m + 1] * total[m : m + 1]
            weight = weight * (1.0 / math.sqrt(ATOMS * LPROJ))
            spread.append(jnp.where(species == s, weight, 0.0))
    nonloc = None
    for s in range(NSPEC):
        at_columns = []
        for weight in spread[LPROJ * s : LPROJ * (s + 1)]:
            around = pltpu.roll(jnp.broadcast_to(weight, (8, 2 * ATOMS)), ATOMS, 1)[0:1]
            at_columns.append(pxy[0] * weight - pxy[1] * around)
        at_columns = jnp.concatenate(at_columns, axis=0)
        spread_z = product(split(at_columns), pz_parts, ((1,), (1,)))
        for q in range(LPROJ):
            factor = pf[s * LPROJ + q]
            part = spread_z[COLS * q : COLS * (q + 1)]
            term = jnp.concatenate([factor * part[:, :COLS], factor * part[:, COLS:]], axis=1)
            nonloc = term if nonloc is None else nonloc + term
        proceed(1)
    row, lane = iota((COLS, COLS), 0), iota((COLS, COLS), 1)
    for c in range(2):
        part = nonloc[:, c * COLS : (c + 1) * COLS]
        extra = jnp.broadcast_to(part[COL_Z : COL_Z + 1, 0:1], (COLS, COLS))
        low = jnp.where((row == 0) & (lane == RADIUS), extra, part)
        nl[c] = jnp.concatenate([low, part], axis=1) + kinetic * xs[c]

    proceed(len(queue))
    recip = None
    for t in range(2):
        landed4[t]()
        term = product(split(jnp.transpose(r4[t])), tz_parts(t))
        recip = term if recip is None else recip + term
    for c in range(2):
        value = jnp.where(inside, nl[c] + recip[:, c * N : (c + 1) * N], 0.0)
        tiles = [value[8 * k : 8 * k + 8] for k in range(16)]
        sub = iota((8, N), 0)
        row = jnp.broadcast_to(value[COL_X : COL_X + 1], (8, N))
        out[c, 4, 0:8, :] = jnp.where(sub == 0, row, 0.0)
        row = jnp.broadcast_to(value[COL_Y : COL_Y + 1], (8, N))
        out[c, 0, 8:16, :] = jnp.where(sub == 0, row, 0.0)
        tiles[8] = jnp.where(sub == COL_Y % 8, 0.0, tiles[8])
        tiles[9] = jnp.where(sub == COL_X % 8, 0.0, tiles[9])
        for k, row in enumerate(ROWS_X):
            out[c, row, 0:8, :] = tiles[2 * k]
            out[c, row, 24:32, :] = tiles[2 * k + 1]
    for sent in (*sent1, *sent4, sent_a1, sent_a2):
        sent()


def per_device(psi_coeff, potential, projectors, coupling, positions, species):
    f32, bf16 = jnp.float32, jnp.bfloat16
    consts = [jnp.asarray(table) for table in tables()]
    hbm = pl.BlockSpec(memory_space=pltpu.HBM)
    vmem = pl.BlockSpec(memory_space=pltpu.VMEM)
    return pl.pallas_call(
        kernel,
        out_shape=pltpu.VMEM((2, 16, 32, N), f32),
        in_specs=[hbm] * 11,
        out_specs=vmem,
        scratch_shapes=[
            pltpu.VMEM((2, 9, 32, N), f32),
            pltpu.VMEM((2, 2, N, 128), f32),
            pltpu.VMEM((NSPEC, LPROJ, 9, 32, N), bf16),
            pltpu.VMEM((LPROJ, NSPEC, LPROJ), f32),
            pltpu.VMEM((3, ATOMS), f32),
            pltpu.VMEM((1, ATOMS), jnp.int32),
            pltpu.VMEM((2, 512, 512), bf16),
            pltpu.VMEM((2, 256, 1024), bf16),
            pltpu.VMEM((2, 1024, 256), bf16),
            pltpu.VMEM((4, 256, 256), bf16),
            pltpu.VMEM((2, 128, 512), f32),
            pltpu.VMEM((2, COLS, N), f32),
            pltpu.VMEM((NSPEC * LPROJ, COLS, COLS), f32),
            pltpu.VMEM((2, 2 * COLS, 2 * ATOMS), bf16),
            pltpu.VMEM((2, COLS, 2 * ATOMS), f32),
            pltpu.VMEM((2, 128, 512), f32),
            pltpu.VMEM((2, COLS, N), f32),
            pltpu.VMEM((2, 256, COLS), f32),
            pltpu.VMEM((2, 256, COLS), f32),
            pltpu.VMEM((2, 256, COLS), f32),
            pltpu.VMEM((2, 256, COLS), f32),
            pltpu.VMEM((2, LPROJ, 128), f32),
            pltpu.VMEM((GX * LPROJ, 128), f32),
            pltpu.VMEM((GY * LPROJ, 128), f32),
            pltpu.SemaphoreType.DMA((14,)),
            pltpu.SemaphoreType.DMA((12,)),
        ],
        compiler_params=pltpu.CompilerParams(
            collective_id=0, has_side_effects=True, vmem_limit_bytes=57 * 1024 * 1024
        ),
    )(
        psi_coeff,
        potential,
        projectors,
        jnp.transpose(coupling, (1, 0, 2)),
        positions,
        species.reshape(1, ATOMS),
        *consts,
    )


def solution(mesh):
    in_specs = (
        P("band", "gx", "gy", None),
        P(("gx", "gy"), None, None),
        P(None, None, "gx", "gy", None),
        P(),
        P(),
        P(),
    )
    out_specs = P("band", "gx", "gy", None)
    return jax.shard_map(
        per_device, mesh=mesh, in_specs=in_specs, out_specs=out_specs, check_vma=False
    )
```

```python
import functools
import math

import jax
import jax.numpy as jnp
import ml_dtypes
import numpy as np
from jax import lax
from jax.experimental import pallas as pl
from jax.experimental.pallas import tpu as pltpu
from jax.sharding import PartitionSpec as P

MESH = pl.DeviceIdType.MESH
N = 256
GX = 16
GY = 8
COLS = 128
RADIUS = 64
ATOMS = 64
NSPEC = 2
LPROJ = 3
TWO_PI = 2.0 * math.pi
ROWS_X = (0, 1, 2, 3, 12, 13, 14, 15)
HELD_X = (0, 1, 2, 3, 5, 6, 7, 8)
COL_Y = 71
COL_X = 72
COL_Z = 73


def column_offsets(col):
    a = col // 16
    b = col % 16
    a = a - 8 * (a >= 4)
    b = b - 16 * (b >= 8)
    a = np.where(col == COL_Y, 0, np.where(col == COL_X, 4, a))
    b = np.where(col == COL_Y, 8, np.where(col == COL_X, 0, b))
    return a, b


def two_parts(table):
    table = table.astype(np.float32)
    high = table.astype(ml_dtypes.bfloat16)
    low = (table - high.astype(np.float32)).astype(ml_dtypes.bfloat16)
    return np.stack([high, low])


@functools.lru_cache(maxsize=None)
def tables():
    t, g, y, c = np.meshgrid(
        np.arange(2), np.arange(GX), np.arange(GY), np.arange(2), indexing="ij"
    )
    z = (16 * g + 2 * y + t).reshape(-1, 1)
    c = c.reshape(-1, 1)
    angle = TWO_PI / N * (z * np.arange(N)[None, :] % N)
    cos, sin = np.cos(angle) / 16, np.sin(angle) / 16
    tz = np.concatenate(
        [np.where(c == 0, cos, sin), np.where(c == 0, -sin, cos)], axis=1
    )
    a, b = column_offsets(np.arange(COLS))
    x0 = np.repeat(np.arange(16), 32)[None, :]
    y0 = np.tile(np.arange(32), 16)[None, :]
    angle = TWO_PI * ((2 * a[:, None] * x0 + b[:, None] * y0) % 32) / 32
    cos, sin = np.cos(angle) / 16, np.sin(angle) / 16
    t1 = np.block([[cos, sin], [-sin, cos]])
    gy = np.repeat(np.arange(GY), GX)[:, None]
    gx = np.tile(np.arange(GX), GY)[:, None]
    angle = TWO_PI * ((gx * x0 + gy * y0) % N) / N
    t2 = np.stack([np.cos(angle), np.sin(angle)]).astype(np.float32)
    y1, x1 = gy, gx
    angle = TWO_PI * ((gx.T * x1 + 2 * gy.T * y1) % 16) / 16
    cos, sin = np.cos(angle) / 16, np.sin(angle) / 16
    e = np.block([[cos, -sin], [sin, cos]])
    return (
        two_parts(tz),
        two_parts(t1),
        two_parts(t1.T),
        np.concatenate([two_parts(e), two_parts(e.T)]),
        t2,
    )


def split(value):
    high = value.astype(jnp.bfloat16)
    return high, (value - high.astype(jnp.float32)).astype(jnp.bfloat16)


def product(left, right, dims=((1,), (0,))):
    def one(first, second):
        return lax.dot_general(
            first, second, (dims, ((), ())), preferred_element_type=jnp.float32
        )

    return one(left[0], right[0]) + (one(left[0], right[1]) + one(left[1], right[0]))


def cos_turns(turns):
    r = (turns - jnp.floor(turns + 0.5)) * math.pi
    r2 = r * r
    s = -1.0 / 39916800.0
    for denom in (362880.0, -5040.0, 120.0, -6.0, 1.0):
        s = s * r2 + 1.0 / denom
    s = s * r
    return 1.0 - 2.0 * s * s


def iota(shape, axis):
    return lax.broadcasted_iota(jnp.int32, shape, axis)


def column_freqs(gx, gy, shape):
    col = iota(shape, 0)
    a = lax.shift_right_logical(col, 4)
    b = col & 15
    a = jnp.where(a >= 4, a - 8, a)
    b = jnp.where(b >= 8, b - 16, b)
    a = jnp.where(col == COL_Y, 0, jnp.where(col == COL_X, 4, a))
    b = jnp.where(col == COL_Y, 8, jnp.where(col == COL_X, 0, b))
    return gx + GX * a, gy + GY * b


def fractional(product_):
    return product_ - jnp.floor(product_)


def inner(value):
    row, lane = iota((COLS, COLS), 0), iota((COLS, COLS), 1)
    both = jnp.where(lane < RADIUS, value[:, :COLS], value[:, COLS:])
    extra = jnp.broadcast_to(value[0:1, RADIUS : RADIUS + 1], (COLS, COLS))
    return jnp.where((row == COL_Z) & (lane == 0), extra, both)


def pick_columns(held):
    tiles = []
    for place, i in enumerate(HELD_X):
        row = held(i)
        first, second = row[0:8], row[24:32]
        if place == 4:
            sub = iota((8, N), 0)
            other = jnp.broadcast_to(held(0)[8:9], (8, N))
            first = jnp.where(sub == 7, other, first)
            other = jnp.broadcast_to(held(4)[0:1], (8, N))
            second = jnp.where(sub == 0, other, second)
        tiles += [first, second]
    return jnp.concatenate(tiles, axis=0)


def kernel(
    psi_h, pot_h, proj_h, coup_h, pos_h, spec_h, tz_h, t1_h, t1t_h, e_h, t2_h,
    out,
    psi, pot, proj, coup, pos, spec, tz, t1, t1t, e, t2,
    xs, pf, pz, pxy, vt, nl,
    zs, r2, s3, r4, ar0, ar1, ar2,
    load_sem, sems,
):
    gx = lax.axis_index("gx")
    gy = lax.axis_index("gy")
    loads = []
    pairs = [
        (psi_h.at[:, 0:5], psi.at[:, 0:5]),
        (psi_h.at[:, 12:16], psi.at[:, 5:9]),
        (tz_h, tz),
        (proj_h.at[:, :, 0:5], proj.at[:, :, 0:5]),
        (proj_h.at[:, :, 12:16], proj.at[:, :, 5:9]),
        (pot_h.at[:, :, 0:128], pot.at[0]),
        (pot_h.at[:, :, 128:256], pot.at[1]),
        (t1_h, t1),
        (t2_h, t2),
        (e_h, e),
        (t1t_h, t1t),
        (pos_h, pos),
        (spec_h, spec),
        (coup_h, coup),
    ]
    for i, (src, dst) in enumerate(pairs):
        loads.append(pltpu.make_async_copy(src, dst, load_sem.at[i]))
    for load in loads[:3]:
        load.start()
    barrier = pltpu.get_barrier_semaphore()
    by_x = [lax.rem(gx + d, GX) for d in range(GX)]
    by_y = [lax.rem(gy + d, GY) for d in range(GY)]

    def greet(px, py):
        pl.semaphore_signal(
            barrier, inc=1, device_id={"gx": px, "gy": py}, device_id_type=MESH
        )

    def greet_rows(j):
        @pl.loop(0, GY)
        def _(d):
            py = lax.rem(gy + d, GY)
            greet(by_x[8 - j], py)
            if j > 0:
                greet(by_x[8 + j], py)

    for j in range(8):
        greet_rows(j)
    for py in by_y[1:]:
        greet(gx, py)
    for load in loads[3:]:
        load.start()

    def exchange(axis, me, count, slot, source, target, block, landing):
        send_sem, recv_sem = sems.at[2 * slot], sems.at[2 * slot + 1]

        def post(d):
            peer = lax.rem(me + d, count)
            pltpu.make_async_remote_copy(
                src_ref=source(peer),
                dst_ref=target(me),
                send_sem=send_sem,
                recv_sem=recv_sem,
                device_id={axis: peer},
                device_id_type=MESH,
            ).start()

        for k in range(1, count):
            d = count // 2 - k // 2 if k % 2 == 1 else count // 2 + k // 2
            post(d)
        pltpu.make_async_copy(source(me), target(me), recv_sem).start()

        def sent():
            pltpu.make_async_copy(block, block, send_sem).wait()

        def landed():
            pltpu.make_async_copy(landing, landing, recv_sem).wait()

        return sent, landed

    def over_x(*args):
        return exchange("gx", gx, GX, *args)

    def over_y(*args):
        return exchange("gy", gy, GY, *args)

    def exchange_all(slot, source, target, source_at, target_at):
        send_sem, recv_sem = sems.at[2 * slot], sems.at[2 * slot + 1]
        mine = target.at[pl.ds(target_at(gx, gy), 2), :]

        def post(px, py):
            pltpu.make_async_remote_copy(
                src_ref=source.at[pl.ds(source_at(px, py), 2), :],
                dst_ref=mine,
                send_sem=send_sem,
                recv_sem=recv_sem,
                device_id={"gx": px, "gy": py},
                device_id_type=MESH,
            ).start()

        def step(j):
            @pl.loop(0, GY)
            def _(d):
                py = lax.rem(gy + d, GY)
                post(by_x[8 - j], py)
                if j > 0:
                    post(by_x[8 + j], py)

        def last():
            for py in by_y[1:]:
                post(gx, py)
            pltpu.make_async_copy(
                source.at[pl.ds(source_at(gx, gy), 2), :], mine, recv_sem
            ).start()

        steps = [functools.partial(step, j) for j in range(8)] + [last]

        def sent():
            block = source.at[pl.ds(0, 254), :]
            pltpu.make_async_copy(block, block, send_sem).wait()

        def landed():
            pltpu.make_async_copy(target, target, recv_sem).wait()

        return steps, sent, landed

    def by_gx(px, py):
        return (px * GY + py) * 2

    def by_gy(px, py):
        return (py * GX + px) * 2

    kx, ky = column_freqs(gx, gy, (COLS, N))
    lane = iota((COLS, N), 1)
    kz = jnp.where(lane < N // 2, lane, lane - N)
    squared = kx * kx + ky * ky + kz * kz
    inside = squared <= RADIUS * RADIUS
    kinetic = squared.astype(jnp.float32) * (1.0 / (RADIUS * RADIUS))
    loads[0].wait()
    loads[1].wait()
    for c in range(2):
        xs[c] = jnp.where(inside, pick_columns(lambda i: psi[c, i]), 0.0)
    x_parts = split(jnp.concatenate([xs[0], xs[1]], axis=1))
    loads[2].wait()

    def tz_parts(t):
        rows = pl.ds(256 * t, 256)
        return tz[0, rows, :], tz[1, rows, :]

    def lines(t):
        zs[t] = product(tz_parts(t), x_parts, ((1,), (1,)))

    def scatter(t):
        return exchange_all(t, zs.at[t], r2.at[t], by_gx, by_gy)

    lines(0)
    pl.semaphore_wait(barrier, GX * GY - 1)
    steps, sent1, landed1 = zip(scatter(0), scatter(1))
    queue = [*steps[0], *steps[1]]

    def proceed(count=1):
        for _ in range(min(count, len(queue))):
            queue.pop(0)()

    proceed(5)
    lines(1)
    for c in range(2):
        for row in range(16):
            if row in ROWS_X:
                out[c, row, 8:24, :] = jnp.zeros((16, N), jnp.float32)
            else:
                out[c, row] = jnp.zeros((32, N), jnp.float32)

    loads[11].wait()
    loads[12].wait()
    loads[13].wait()
    atoms2 = jnp.concatenate([pos[...], pos[...]], axis=1)
    half = iota((1, 2 * ATOMS), 1) >= ATOMS
    quarter = jnp.where(half, 0.25, 0.0)
    row = iota((COLS, 2 * ATOMS), 0)
    kz_rows = jnp.where(row < RADIUS, row, row - 2 * RADIUS).astype(jnp.float32)
    turns_z = fractional(kz_rows * atoms2[2:3])
    pz_f32 = jnp.concatenate(
        [cos_turns(turns_z - quarter), cos_turns(turns_z + (0.25 - quarter))], axis=0
    )
    pz[0], pz[1] = split(pz_f32)
    proceed()
    kx_col, ky_col = column_freqs(gx, gy, (COLS, 2 * ATOMS))
    turns_xy = fractional(kx_col.astype(jnp.float32) * atoms2[0:1]) + fractional(
        ky_col.astype(jnp.float32) * atoms2[1:2]
    )
    turns_xy = jnp.where(row == COL_Z, fractional(RADIUS * atoms2[2:3]), turns_xy)
    pxy[0] = cos_turns(turns_xy)
    pxy[1] = cos_turns(turns_xy + jnp.where(half, -0.25, 0.25))
    proceed()

    loads[3].wait()
    loads[4].wait()
    pz_parts = (pz[0], pz[1])
    inner_re, inner_im = inner(xs[0]), inner(xs[1])
    sums = []
    for s in range(NSPEC):
        weighted = []
        for q in range(LPROJ):
            factor = inner(pick_columns(lambda i: proj[s, q, i].astype(jnp.float32)))
            pf[s * LPROJ + q] = factor
            weighted.append(jnp.concatenate([factor * inner_re, factor * inner_im], axis=1))
            proceed(3)
        along_z = product(split(jnp.concatenate(weighted, axis=0)), pz_parts)
        for q in range(LPROJ):
            part = along_z[COLS * q : COLS * (q + 1)]
            along = part * pxy[0] + pltpu.roll(part, ATOMS, 1) * pxy[1]
            sums.append(jnp.sum(along, axis=0, keepdims=True))
    species = jnp.concatenate([spec[...], spec[...]], axis=1)
    norm = 4.0 / math.sqrt(N * N * N)
    for q in range(LPROJ):
        ar0[0, q : q + 1, :] = jnp.where(species == 0, sums[q], sums[LPROJ + q]) * norm
    sent_a1, landed_a1 = over_x(
        4, lambda p: ar0.at[0], lambda m: ar1.at[pl.ds(LPROJ * m, LPROJ), :],
        ar1.at[pl.ds(0, LPROJ * (GX - 1)), :], ar1,
    )

    loads[5].wait()
    loads[6].wait()
    lane16 = iota((16, 128), 1)
    for t in range(2):
        for block in range(4):
            for hy in range(2):
                strips = [
                    pot[hy, t, pl.ds(4 * block + j, 16, stride=16), :] for j in range(4)
                ]
                for r in range(4):
                    tile = None
                    for j in range(4):
                        shift = (32 * (j - r)) % 128
                        moved = strips[j] if shift == 0 else pltpu.roll(strips[j], shift, 1)
                        tile = moved if tile is None else jnp.where(lane16 >= 32 * j, moved, tile)
                    y1 = 4 * hy + r
                    vt[t, pl.ds(16 * y1, 16), pl.ds(128 * block, 128)] = tile
        proceed(1)

    def plane(t):
        landed1[t]()
        values = jnp.concatenate(
            [r2[t, pl.ds(0, COLS, stride=2), :], r2[t, pl.ds(1, COLS, stride=2), :]], axis=1
        )
        lanes = product(split(values), (t1[0], t1[1]))
        proceed(2)
        lanes_re, lanes_im = lanes[:, :512], lanes[:, 512:]
        cos, sin = t2[0], t2[1]
        turned = jnp.concatenate(
            [lanes_re * cos - lanes_im * sin, lanes_re * sin + lanes_im * cos], axis=0
        )
        space = product((e[0], e[1]), split(turned))
        proceed(2)
        field = jnp.concatenate([space[:128] * vt[t], space[128:] * vt[t]], axis=0)
        rows = product((e[2], e[3]), split(field))
        proceed(2)
        rows_re, rows_im = rows[:128], rows[128:]
        turned = jnp.concatenate(
            [rows_re * cos + rows_im * sin, rows_im * cos - rows_re * sin], axis=1
        )
        back = product(split(turned), (t1t[0], t1t[1]))
        s3[t, pl.ds(0, COLS, stride=2), :] = back[:, :128]
        s3[t, pl.ds(1, COLS, stride=2), :] = back[:, 128:]

    def gather(t):
        return exchange_all(2 + t, s3.at[t], r4.at[t], by_gy, by_gx)

    steps4, sent4, landed4 = zip(gather(0), gather(1))
    for i in range(7, 11):
        loads[i].wait()
    proceed(9)
    plane(0)
    proceed(len(queue))
    queue += steps4[0]
    proceed(9)
    landed_a1()
    total = ar1[0:LPROJ, :]
    for g in range(1, GX):
        total += ar1[LPROJ * g : LPROJ * (g + 1), :]
    ar0[1] = total
    sent_a2, landed_a2 = over_y(
        5, lambda p: ar0.at[1], lambda m: ar2.at[pl.ds(LPROJ * m, LPROJ), :],
        ar2.at[pl.ds(0, LPROJ * (GY - 1)), :], ar2,
    )
    proceed(9)
    plane(1)
    proceed(len(queue))
    queue += steps4[1]
    proceed(9)

    landed_a2()
    total = ar2[0:LPROJ, :]
    for g in range(1, GY):
        total += ar2[LPROJ * g : LPROJ * (g + 1), :]
    spread = []
    for s in range(NSPEC):
        for q in range(LPROJ):
            weight = coup[q, s : s + 1, 0:1] * total[0:1]
            for m in range(1, LPROJ):
                weight += coup[q, s : s + 1, m : m + 1] * total[m : m + 1]
            weight = weight * (1.0 / math.sqrt(ATOMS * LPROJ))
            spread.append(jnp.where(species == s, weight, 0.0))
    nonloc = None
    for s in range(NSPEC):
        at_columns = []
        for weight in spread[LPROJ * s : LPROJ * (s + 1)]:
            around = pltpu.roll(jnp.broadcast_to(weight, (8, 2 * ATOMS)), ATOMS, 1)[0:1]
            at_columns.append(pxy[0] * weight - pxy[1] * around)
        at_columns = jnp.concatenate(at_columns, axis=0)
        spread_z = product(split(at_columns), pz_parts, ((1,), (1,)))
        for q in range(LPROJ):
            factor = pf[s * LPROJ + q]
            part = spread_z[COLS * q : COLS * (q + 1)]
            term = jnp.concatenate([factor * part[:, :COLS], factor * part[:, COLS:]], axis=1)
            nonloc = term if nonloc is None else nonloc + term
        proceed(1)
    row, lane = iota((COLS, COLS), 0), iota((COLS, COLS), 1)
    for c in range(2):
        part = nonloc[:, c * COLS : (c + 1) * COLS]
        extra = jnp.broadcast_to(part[COL_Z : COL_Z + 1, 0:1], (COLS, COLS))
        low = jnp.where((row == 0) & (lane == RADIUS), extra, part)
        nl[c] = jnp.concatenate([low, part], axis=1) + kinetic * xs[c]

    proceed(len(queue))
    recip = None
    for t in range(2):
        landed4[t]()
        term = product(split(jnp.transpose(r4[t])), tz_parts(t))
        recip = term if recip is None else recip + term
    for c in range(2):
        value = jnp.where(inside, nl[c] + recip[:, c * N : (c + 1) * N], 0.0)
        tiles = [value[8 * k : 8 * k + 8] for k in range(16)]
        sub = iota((8, N), 0)
        row = jnp.broadcast_to(value[COL_X : COL_X + 1], (8, N))
        out[c, 4, 0:8, :] = jnp.where(sub == 0, row, 0.0)
        row = jnp.broadcast_to(value[COL_Y : COL_Y + 1], (8, N))
        out[c, 0, 8:16, :] = jnp.where(sub == 0, row, 0.0)
        tiles[8] = jnp.where(sub == COL_Y % 8, 0.0, tiles[8])
        tiles[9] = jnp.where(sub == COL_X % 8, 0.0, tiles[9])
        for k, row in enumerate(ROWS_X):
            out[c, row, 0:8, :] = tiles[2 * k]
            out[c, row, 24:32, :] = tiles[2 * k + 1]
    for sent in (*sent1, *sent4, sent_a1, sent_a2):
        sent()


def per_device(psi_coeff, potential, projectors, coupling, positions, species):
    f32, bf16 = jnp.float32, jnp.bfloat16
    consts = [jnp.asarray(table) for table in tables()]
    hbm = pl.BlockSpec(memory_space=pltpu.HBM)
    vmem = pl.BlockSpec(memory_space=pltpu.VMEM)
    return pl.pallas_call(
        kernel,
        out_shape=pltpu.VMEM((2, 16, 32, N), f32),
        in_specs=[hbm] * 11,
        out_specs=vmem,
        scratch_shapes=[
            pltpu.VMEM((2, 9, 32, N), f32),
            pltpu.VMEM((2, 2, N, 128), f32),
            pltpu.VMEM((NSPEC, LPROJ, 9, 32, N), bf16),
            pltpu.VMEM((LPROJ, NSPEC, LPROJ), f32),
            pltpu.VMEM((3, ATOMS), f32),
            pltpu.VMEM((1, ATOMS), jnp.int32),
            pltpu.VMEM((2, 512, 512), bf16),
            pltpu.VMEM((2, 256, 1024), bf16),
            pltpu.VMEM((2, 1024, 256), bf16),
            pltpu.VMEM((4, 256, 256), bf16),
            pltpu.VMEM((2, 128, 512), f32),
            pltpu.VMEM((2, COLS, N), f32),
            pltpu.VMEM((NSPEC * LPROJ, COLS, COLS), f32),
            pltpu.VMEM((2, 2 * COLS, 2 * ATOMS), bf16),
            pltpu.VMEM((2, COLS, 2 * ATOMS), f32),
            pltpu.VMEM((2, 128, 512), f32),
            pltpu.VMEM((2, COLS, N), f32),
            pltpu.VMEM((2, 256, COLS), f32),
            pltpu.VMEM((2, 256, COLS), f32),
            pltpu.VMEM((2, 256, COLS), f32),
            pltpu.VMEM((2, 256, COLS), f32),
            pltpu.VMEM((2, LPROJ, 128), f32),
            pltpu.VMEM((GX * LPROJ, 128), f32),
            pltpu.VMEM((GY * LPROJ, 128), f32),
            pltpu.SemaphoreType.DMA((14,)),
            pltpu.SemaphoreType.DMA((12,)),
        ],
        compiler_params=pltpu.CompilerParams(
            collective_id=0, has_side_effects=True, vmem_limit_bytes=57 * 1024 * 1024
        ),
    )(
        psi_coeff,
        potential,
        projectors,
        jnp.transpose(coupling, (1, 0, 2)),
        positions,
        species.reshape(1, ATOMS),
        *consts,
    )


def solution(mesh):
    in_specs = (
        P("band", "gx", "gy", None),
        P(("gx", "gy"), None, None),
        P(None, None, "gx", "gy", None),
        P(),
        P(),
        P(),
    )
    out_specs = P("band", "gx", "gy", None)
    return jax.shard_map(
        per_device, mesh=mesh, in_specs=in_specs, out_specs=out_specs, check_vma=False
    )
```
